256 devices in a mesh: gx: 8 (over y, core), gy: 32 (over z, x).
Axes of the slice: x: 4, y: 4, z: 8, core: 2. Of those that a mesh axis runs over, the one named last changes fastest.
Arguments:
- motion_cotangent: float32 [3, 128, 512, 512], P(None, 'gx', 'gy'), may hold values from -8 to 8
- scaled_warmth: float32 [128, 512, 512], P('gx', 'gy'), may hold values from 0 to 1
- yielding_flags: int32 [128, 512, 512], P('gx', 'gy'), may hold values 0 or 1
- printed_flags: int32 [128, 512, 512], P('gx', 'gy'), may hold values 0 or 1
- material_label: int32 [128, 512, 512], P('gx', 'gy'), may hold values from 0 to 3
- phase_rigidity: float32 [4], replicated, may hold values from 0.5 to 4
- phase_dilatation: float32 [4], replicated, may hold values from 0.5 to 2
- phase_diffusivity: float32 [4], replicated, may hold values from 0.2 to 1
Outputs:
- adjoint_displacement: float32 [3, 128, 512, 512], P(None, 'gx', 'gy')
- thermal_adjoint: float32 [128, 512, 512], P('gx', 'gy')
The draws below stay inside these ranges and needn't reach their ends.
All inputs are finite; a program needn't handle non-finite values. No bound on the sum of `yielding_flags` or of `printed_flags` on one device may be relied on, other than what follows from the above.
Results may differ from the reference program's by a relative error of at most 0.0001.
Values sent between devices are 32-bit elements; how exact they have to be, the bound alone decides.
A program may use at most 64 MiB of HBM per device.

```python
import math
import jax
import jax.numpy as jnp

POINTS_THIRD_DIM = 512
ITERS = 2
PHASES = 4
POINTS_FIRST_DIM = 128
POINTS_SECOND_DIM = 512


def draw_motion_cotangent(key, part):
    subkeys = jax.random.split(jax.random.fold_in(key, 17), 7)
    full_shape = (3, POINTS_FIRST_DIM, POINTS_SECOND_DIM, POINTS_THIRD_DIM)
    background = jax.random.normal(subkeys[0], full_shape, jnp.float32)
    shared_sign = jax.random.rademacher(subkeys[1], (3, 1, 1, 1), jnp.float32)
    shared_depth = jax.random.uniform(subkeys[2], (1, 1, 1, POINTS_THIRD_DIM), jnp.float32, 0.3, 0.6)
    row_signs = jax.random.rademacher(subkeys[3], (3, POINTS_FIRST_DIM, 1, 1), jnp.float32)
    column_signs = jax.random.rademacher(subkeys[4], (3, 1, POINTS_SECOND_DIM, 1), jnp.float32)
    depth_sign = jax.random.rademacher(subkeys[5], (3, 1, 1, POINTS_THIRD_DIM), jnp.float32)
    depth_size = jax.random.uniform(subkeys[6], (3, 1, 1, POINTS_THIRD_DIM), jnp.float32, 0.6, 1.0)
    layered = row_signs * column_signs * depth_sign * depth_size
    total = background + shared_sign * shared_depth + layered
    return jnp.clip(total, -8.0, 8.0).astype(jnp.float32)


def plant(array, key, low, top_value):
    place = [jax.random.randint(jax.random.fold_in(key, axis), (), 0, length) for axis, length in enumerate(array.shape)]
    main_axis = array.shape.index(max(array.shape))
    neighbour = place[:main_axis] + [(place[main_axis] + 1) % array.shape[main_axis]] + place[main_axis + 1:]
    return array.at[tuple(place)].set(low).at[tuple(neighbour)].set(top_value)


def block_scale(stream_key, extent, shards, low, largest):
    def one(axis_at, blocks):
        steps = jax.random.uniform(jax.random.fold_in(jax.random.fold_in(stream_key, 6), axis_at), (blocks,), jnp.float32, low / len(shards), largest / len(shards))
        return jnp.repeat(jnp.exp(steps), extent[axis_at] // blocks).reshape((-1,) + (1,) * (len(extent) - axis_at - 1))

    factor_of = one(*shards[0])
    for cut in shards[1:]:
        factor_of = factor_of * one(*cut)
    return factor_of


def setup_inputs(seed: int = 0) -> dict:
    arg_keys = jax.random.split(jax.random.key(seed), 9)
    motion_cotangent = draw_motion_cotangent(jax.random.fold_in(arg_keys[8], 71), 0)
    scaled_warmth = jnp.clip(1.0 * jax.random.uniform(arg_keys[1], (POINTS_FIRST_DIM, POINTS_SECOND_DIM, POINTS_THIRD_DIM), jnp.float32) ** block_scale(arg_keys[1], (POINTS_FIRST_DIM, POINTS_SECOND_DIM, POINTS_THIRD_DIM), ((0, 8), (1, 32)), -0.2, 0.2), 0.0, 1.0)
    yielding_flags = plant((jax.random.randint(arg_keys[2], (POINTS_FIRST_DIM, POINTS_SECOND_DIM, POINTS_THIRD_DIM), 0, 3) < 1).astype(jnp.int32), jax.random.fold_in(arg_keys[2], 1), 0, 1)
    printed_flags = plant((jax.random.randint(arg_keys[3], (POINTS_FIRST_DIM, POINTS_SECOND_DIM, POINTS_THIRD_DIM), 0, 4) < 3).astype(jnp.int32), jax.random.fold_in(arg_keys[3], 1), 0, 1)
    material_label = plant(jax.random.randint(arg_keys[4], (POINTS_FIRST_DIM, POINTS_SECOND_DIM, POINTS_THIRD_DIM), 0, PHASES), jax.random.fold_in(arg_keys[4], 1), 0, PHASES - 1).astype(jnp.int32)
    phase_rigidity = jnp.clip(jnp.exp(jax.random.uniform(arg_keys[5], (PHASES,), jnp.float32, math.log(0.5), math.log(4.0))), 0.5, 4.0)
    phase_dilatation = jnp.clip(jnp.exp(jax.random.uniform(arg_keys[6], (PHASES,), jnp.float32, math.log(0.5), math.log(2.0))), 0.5, 2.0)
    phase_diffusivity = jnp.clip(jnp.exp(jax.random.uniform(arg_keys[7], (PHASES,), jnp.float32, math.log(0.2), math.log(1.0))), 0.2, 1.0)
    return dict(motion_cotangent=motion_cotangent, scaled_warmth=scaled_warmth, yielding_flags=yielding_flags, printed_flags=printed_flags, material_label=material_label, phase_rigidity=phase_rigidity, phase_dilatation=phase_dilatation, phase_diffusivity=phase_diffusivity)


def pad_three(field):
    widths = [(0, 0)] * (field.ndim - 3) + [(1, 1)] * 3
    return jnp.pad(field, widths)


def neighbours(padded):
    return [padded[..., 2:, 1:-1, 1:-1], padded[..., :-2, 1:-1, 1:-1],
            padded[..., 1:-1, 2:, 1:-1], padded[..., 1:-1, :-2, 1:-1],
            padded[..., 1:-1, 1:-1, 2:], padded[..., 1:-1, 1:-1, :-2]]


def reference(motion_cotangent, scaled_warmth, yielding_flags, printed_flags, material_label, phase_rigidity, phase_dilatation, phase_diffusivity):
    hooke_tensor = jnp.take(phase_rigidity, material_label) * (1.0 - 0.7 * yielding_flags.astype(jnp.float32)) * (0.05 + 0.95 * printed_flags.astype(jnp.float32))
    conductance = jnp.take(phase_diffusivity, material_label)
    weights = [0.5 * (hooke_tensor + other) for other in neighbours(pad_three(hooke_tensor))]
    diagonal = 0.5 + sum(weights)

    def operate(field):
        beside_all = neighbours(pad_three(field))
        total = diagonal * field
        for weight, other in zip(weights, beside_all):
            total = total - weight * other
        return total

    solution = jnp.zeros_like(motion_cotangent)
    residual = motion_cotangent
    direction = motion_cotangent
    norm_now = jnp.sum(residual * residual)
    for iteration in range(ITERS):
        applied = operate(direction)
        step_size = norm_now / jnp.sum(direction * applied)
        solution = solution + step_size * direction
        residual = residual - step_size * applied
        norm_next = jnp.sum(residual * residual)
        direction = residual + (norm_next / norm_now) * direction
        norm_now = norm_next
    padded = pad_three(solution)
    flux_balance = padded[0, 2:, 1:-1, 1:-1] - padded[0, :-2, 1:-1, 1:-1]
    flux_balance = flux_balance + (padded[1, 1:-1, 2:, 1:-1] - padded[1, 1:-1, :-2, 1:-1])
    flux_balance = flux_balance + (padded[2, 1:-1, 1:-1, 2:] - padded[2, 1:-1, 1:-1, :-2])
    energy_input = -0.5 * jnp.take(phase_dilatation, material_label) * (0.5 + scaled_warmth) * hooke_tensor * flux_balance
    cond_near = neighbours(pad_three(conductance))
    source_near = neighbours(pad_three(energy_input))
    change = jnp.zeros_like(energy_input)
    for other_c, other_s in zip(cond_near, source_near):
        change = change + 0.5 * (conductance + other_c) * (other_s - energy_input)
    thermal = energy_input + 0.15 * change
    return solution, thermal
```

```python
import functools

import jax
import jax.numpy as jnp
from jax import lax
from jax.experimental import pallas as pl
from jax.experimental.pallas import tpu as pltpu
from jax.sharding import PartitionSpec as P

MESH = pl.DeviceIdType.MESH
RING_X = 4


def pick(table, label):
    low = jnp.where(label == 0, table[0], table[1])
    high = jnp.where(label == 2, table[2], table[3])
    return jnp.where(label < 2, low, high)


def fold(plane):
    rows, lanes = plane.shape
    total = None
    for i in range(0, rows, 8):
        for j in range(0, lanes, 128):
            part = plane[i : i + 8, j : j + 128]
            total = part if total is None else total + part
    return total


def kernel(
    gx_size, gy_size,
    b_hbm, warm_hbm, yield_hbm, print_hbm, label_hbm, rigidity, dilatation, diffusivity,
    x_out, th_out,
    B, U, H, WARM, YIELD, PRINT, LABEL, TS, WY, WZ, D, S3, T,
    y1_lo, y1_hi, r1_lo, r1_hi,
    y2_lo, y2_hi, r2_lo, r2_hi,
    y3_lo, y3_hi, r3_lo, r3_hi,
    sums,
    load_sem, send1, recv1, send2, recv2, send3, recv3, send_r, recv_r,
):
    _, nx, ny, nz = b_hbm.shape
    gx, gy = lax.axis_index("gx"), lax.axis_index("gy")
    ring_z = gy_size // RING_X
    gz, gq = gy // RING_X, gy % RING_X
    up_x, down_x = (gx + 1) % gx_size, (gx + gx_size - 1) % gx_size
    up_y, down_y = (gy + 1) % gy_size, (gy + gy_size - 1) % gy_size
    stages = []
    for stage, count in enumerate((gx_size, ring_z, RING_X)):
        partners = []
        for k in range(1, count):
            if stage == 0:
                partners.append(((gx + k) % gx_size, gy))
            elif stage == 1:
                partners.append((gx, ((gz + k) % ring_z) * RING_X + gq))
            else:
                partners.append((gx, gz * RING_X + (gq + k) % RING_X))
        stages.append(partners)

    loads = [
        pltpu.make_async_copy(label_hbm, LABEL, load_sem.at[0]),
        pltpu.make_async_copy(yield_hbm, YIELD, load_sem.at[1]),
        pltpu.make_async_copy(print_hbm, PRINT, load_sem.at[2]),
        pltpu.make_async_copy(warm_hbm, WARM, load_sem.at[3]),
        pltpu.make_async_copy(b_hbm, B.at[:, pl.ds(1, nx)], load_sem.at[4]),
    ]
    for load in loads:
        load.start()

    barrier = pltpu.get_barrier_semaphore()
    greeted = [(up_x, gy), (down_x, gy), (gx, up_y), (gx, down_y)]
    for partners in stages:
        greeted += partners
    for partner in greeted:
        pl.semaphore_signal(barrier, inc=1, device_id=partner, device_id_type=MESH)

    row = lax.broadcasted_iota(jnp.int32, (ny, nz), 0)
    lane = lax.broadcasted_iota(jnp.int32, (ny, nz), 1)
    first_row, last_row = row == 0, row == ny - 1
    last_lane = lane == nz - 1
    edge_lane = (lane == 0) | last_lane

    def remote(src, dst, send, recv, partner):
        return pltpu.make_async_remote_copy(
            src_ref=src, dst_ref=dst, send_sem=send, recv_sem=recv,
            device_id=partner, device_id_type=MESH,
        )

    def faces(field, ylo, yhi, rlo, rhi, send, recv, base):
        lead = (slice(None),) * (len(field.shape) - 3)
        at = lambda i: field.at[lead + (i,)]
        return [
            remote(at(nx), at(0), send.at[base], recv.at[base], (up_x, gy)),
            remote(at(1), at(nx + 1), send.at[base + 1], recv.at[base + 1], (down_x, gy)),
            remote(yhi, rlo, send.at[base + 2], recv.at[base + 2], (gx, up_y)),
            remote(ylo, rhi, send.at[base + 3], recv.at[base + 3], (gx, down_y)),
        ]

    for load in loads:
        load.wait()

    def properties(x, carry):
        label = LABEL[x]
        stiffness = (
            pick(rigidity, label)
            * (1.0 - 0.7 * YIELD[x].astype(jnp.float32))
            * (0.05 + 0.95 * PRINT[x].astype(jnp.float32))
        )
        half = 0.5 * stiffness
        H[x + 1] = half
        TS[x] = pick(dilatation, label) * (0.5 + WARM[x]) * half
        half_c = 0.5 * pick(diffusivity, label)
        S3[2, x + 1] = half_c
        at = pl.ds(x, 1)
        for c in range(3):
            y1_lo[c, at, :] = B[c, x + 1, 0:1, :]
            y1_hi[c, at, :] = B[c, x + 1, ny - 1 : ny, :]
        y1_lo[3, at, :] = half[0:1, :]
        y1_hi[3, at, :] = half[ny - 1 : ny, :]
        y3_lo[2, at, :] = half_c[0:1, :]
        y3_hi[2, at, :] = half_c[ny - 1 : ny, :]
        return carry

    lax.fori_loop(0, nx, properties, 0)

    pl.semaphore_wait(barrier, len(greeted))

    copies1 = faces(B, y1_lo, y1_hi, r1_lo, r1_hi, send1, recv1, 0)
    copies1 += [
        remote(H.at[nx], H.at[0], send1.at[4], recv1.at[4], (up_x, gy)),
        remote(H.at[1], H.at[nx + 1], send1.at[5], recv1.at[5], (down_x, gy)),
    ]
    for copy in copies1:
        copy.start()
    for copy in copies1:
        copy.wait()

    def clear(field, rlo, rhi):
        lead = (slice(None),) * (len(field.shape) - 3)

        @pl.when(gx == 0)
        def _():
            field[lead + (0,)] = jnp.zeros(field.shape[:-3] + (ny, nz), jnp.float32)

        @pl.when(gx == gx_size - 1)
        def _():
            field[lead + (nx + 1,)] = jnp.zeros(field.shape[:-3] + (ny, nz), jnp.float32)

        if rlo is None:
            return

        @pl.when(gy == 0)
        def _():
            rlo[...] = jnp.zeros(rlo.shape, jnp.float32)

        @pl.when(gy == gy_size - 1)
        def _():
            rhi[...] = jnp.zeros(rhi.shape, jnp.float32)

    clear(B, r1_lo, r1_hi)
    clear(H, None, None)

    def next_y(plane, row_hi):
        return jnp.where(last_row, row_hi, pltpu.roll(plane, ny - 1, 0))

    def prev_y(plane, row_lo):
        return jnp.where(first_row, row_lo, pltpu.roll(plane, 1, 0))

    def next_z(plane):
        return pltpu.roll(plane, nz - 1, 1)

    def prev_z(plane):
        return pltpu.roll(plane, 1, 1)

    def inflow(here, below, above, row_lo, row_hi, wxm, wxp, wy, wz, wlo):
        total = wxp * (above - here) + wxm * (below - here)
        flux = wy * (next_y(here, row_hi) - here)
        total += flux - prev_y(flux, wlo * (here[0:1, :] - row_lo))
        flux = wz * (next_z(here) - here)
        return total + (flux - prev_z(flux))

    zero = jnp.zeros((8, 128), jnp.float32)

    def first_image(x, carry):
        bu, uu = carry
        at = pl.ds(x, 1)
        half = H[x + 1]
        wxp, wxm = half + H[x + 2], half + H[x]
        wlo = half[0:1, :] + r1_lo[3, at, :]
        wy = half + next_y(half, r1_hi[3, at, :])
        wz = jnp.where(last_lane, 0.0, half + next_z(half))
        diag = 0.5 + jnp.where(edge_lane, half, 0.0)
        WY[x], WZ[x], D[x] = wy, wz, diag
        for c in range(3):
            here = B[c, x + 1]
            image = diag * here - inflow(
                here, B[c, x], B[c, x + 2], r1_lo[c, at, :], r1_hi[c, at, :],
                wxm, wxp, wy, wz, wlo,
            )
            U[c, x + 1] = image
            y2_lo[c, at, :] = image[0:1, :]
            y2_hi[c, at, :] = image[ny - 1 : ny, :]
            bu += fold(here * image)
            uu += fold(image * image)
        return bu, uu

    bu, uu = lax.fori_loop(0, nx, first_image, (zero, zero))

    copies2 = faces(U, y2_lo, y2_hi, r2_lo, r2_hi, send2, recv2, 0)
    for copy in copies2:
        copy.start()

    def everywhere(tile):
        total = jnp.sum(jnp.sum(tile, axis=0, keepdims=True), axis=1, keepdims=True)
        return jnp.broadcast_to(total, (1, 128))

    weight = everywhere(uu)
    sigma = everywhere(bu) / jnp.where(weight > 0.0, weight, 1.0)

    def source_of(field, rlo, rhi, out, ylo, yhi):
        def body(x, carry):
            at = pl.ds(x, 1)
            mid, last = field[1, x + 1], field[2, x + 1]
            div = field[0, x + 2] - field[0, x]
            div += next_y(mid, rhi[1, at, :]) - prev_y(mid, rlo[1, at, :])
            div += jnp.where(last_lane, 0.0, next_z(last)) - jnp.where(lane == 0, 0.0, prev_z(last))
            source = -TS[x] * div
            S3[out, x + 1] = source
            ylo[out, at, :] = source[0:1, :]
            yhi[out, at, :] = source[ny - 1 : ny, :]
            return carry

        lax.fori_loop(0, nx, body, 0)

    source_of(B, r1_lo, r1_hi, 0, y3_lo, y3_hi)

    for copy in copies2:
        copy.wait()
    clear(U, r2_lo, r2_hi)

    sigma_all = jnp.broadcast_to(sigma[:, 0:1], (ny, nz))

    def second_image(x, carry):
        rr, ru, rv, uv = carry
        at = pl.ds(x, 1)
        half = H[x + 1]
        wxp, wxm = half + H[x + 2], half + H[x]
        wlo = half[0:1, :] + r1_lo[3, at, :]
        wy, wz, diag = WY[x], WZ[x], D[x]
        for c in range(3):
            here = U[c, x + 1]
            image = diag * here - inflow(
                here, U[c, x], U[c, x + 2], r2_lo[c, at, :], r2_hi[c, at, :],
                wxm, wxp, wy, wz, wlo,
            )
            rest = B[c, x + 1] - sigma_all * here
            rr += fold(rest * rest)
            ru += fold(rest * here)
            rv += fold(rest * image)
            uv += fold(here * image)
        return rr, ru, rv, uv

    moments = lax.fori_loop(0, nx, second_image, (zero,) * 4)

    def lanes(tile):
        return jnp.sum(tile, axis=0, keepdims=True)

    def pack(parts):
        index = lax.broadcasted_iota(jnp.int32, (8, 128), 0)
        tile = jnp.zeros((8, 128), jnp.float32)
        for i, part in enumerate(parts):
            tile = jnp.where(index == i, jnp.broadcast_to(part, (8, 128)), tile)
        return tile

    def merge(tiles):
        rows = [[tile[i : i + 1, :] for i in range(7)] for tile in tiles]
        weight = sum(r[6] for r in rows)
        sigma = sum(r[6] * r[5] for r in rows) / jnp.where(weight > 0.0, weight, 1.0)
        out = [0.0] * 5
        for uu, rr, ru, rv, uv, own, _ in rows:
            tau = own - sigma
            shifted = (
                uu, rr + tau * (2.0 * ru + tau * uu), ru + tau * uu, rv + tau * uv, uv,
            )
            out = [a + b for a, b in zip(out, shifted)]
        return out + [sigma, weight]

    state = [lanes(uu)] + [lanes(m) for m in moments] + [sigma, weight]

    def reduce_start(stage, state):
        base = sum(len(s) for s in stages[:stage])
        own = sums.at[base + stage]
        sums[base + stage] = pack(state)
        copies = []
        for k, partner in enumerate(stages[stage]):
            copies.append(
                remote(own, sums.at[base + stage + 1 + k], send_r.at[base + k], recv_r.at[base + k], partner)
            )
        for copy in copies:
            copy.start()
        return copies

    def reduce_finish(stage, copies):
        base = sum(len(s) for s in stages[:stage]) + stage
        for copy in copies:
            copy.wait()
        return merge([sums[base + k] for k in range(len(copies) + 1)])

    pending = reduce_start(0, state)
    source_of(U, r2_lo, r2_hi, 1, y3_lo, y3_hi)
    copies3 = faces(S3, y3_lo, y3_hi, r3_lo, r3_hi, send3, recv3, 0)
    for copy in copies3:
        copy.start()
    state = reduce_finish(0, pending)
    pending = reduce_start(1, state)
    for copy in copies3:
        copy.wait()
    clear(S3, r3_lo, r3_hi)
    state = reduce_finish(1, pending)
    pending = reduce_start(2, state)

    def conduct(x, carry):
        at = pl.ds(x, 1)
        half = S3[2, x + 1]
        wxp, wxm = half + S3[2, x + 2], half + S3[2, x]
        wlo = half[0:1, :] + r3_lo[2, at, :]
        wy = half + next_y(half, r3_hi[2, at, :])
        wz = jnp.where(last_lane, 0.0, half + next_z(half))
        diag = 1.0 - 0.15 * jnp.where(edge_lane, half, 0.0)
        for c in range(2):
            here = S3[c, x + 1]
            T[c, x] = diag * here + 0.15 * inflow(
                here, S3[c, x], S3[c, x + 2], r3_lo[c, at, :], r3_hi[c, at, :],
                wxm, wxp, wy, wz, wlo,
            )
        return carry

    lax.fori_loop(0, nx, conduct, 0)
    state = reduce_finish(2, pending)

    uu, rr, ru, rv, uv, sigma = [
        jnp.sum(part, axis=1, keepdims=True) for part in state[:5]
    ] + [state[5][:, 0:1]]
    energy = ru + sigma * uu
    norm = rr + sigma * (2.0 * ru + sigma * uu)
    step0 = norm / energy
    tau = sigma - step0
    norm1 = rr + tau * (2.0 * ru + tau * uu)
    ru, rv = ru + tau * uu, rv + tau * uv
    ratio = norm1 / norm
    curve = (ru - step0 * rv) + ratio * (2.0 * ru + ratio * energy)
    step1 = norm1 / curve
    coef_b = jnp.broadcast_to(step0 + step1 * (1.0 + ratio), (ny, nz))
    coef_u = jnp.broadcast_to(-step1 * step0, (ny, nz))

    def combine(x, carry):
        for c in range(3):
            x_out[c, x] = coef_b * B[c, x + 1] + coef_u * U[c, x + 1]
        th_out[x] = coef_b * T[0, x] + coef_u * T[1, x]
        return carry

    lax.fori_loop(0, nx, combine, 0)


def per_device(*args):
    b = args[0]
    _, nx, ny, nz = b.shape
    gx_size, gy_size = lax.axis_size("gx"), lax.axis_size("gy")
    partners = gx_size - 1 + gy_size // RING_X - 1 + RING_X - 1
    f32 = jnp.float32
    plane = (ny, nz)
    face = (nx, nz)
    hbm, smem, vmem = (
        pl.BlockSpec(memory_space=m) for m in (pl.ANY, pltpu.SMEM, pltpu.VMEM)
    )
    dma = pltpu.SemaphoreType.DMA
    scratch = [
        pltpu.VMEM((3, nx + 2) + plane, f32),
        pltpu.VMEM((3, nx + 2) + plane, f32),
        pltpu.VMEM((nx + 2,) + plane, f32),
        pltpu.VMEM((nx,) + plane, f32),
        pltpu.VMEM((nx,) + plane, jnp.int32),
        pltpu.VMEM((nx,) + plane, jnp.int32),
        pltpu.VMEM((nx,) + plane, jnp.int32),
        pltpu.VMEM((nx,) + plane, f32),
        pltpu.VMEM((nx,) + plane, f32),
        pltpu.VMEM((nx,) + plane, f32),
        pltpu.VMEM((nx,) + plane, f32),
        pltpu.VMEM((3, nx + 2) + plane, f32),
        pltpu.VMEM((2, nx) + plane, f32),
    ]
    for fields in (4, 3, 3):
        scratch += [pltpu.VMEM((fields,) + face, f32)] * 4
    scratch += [
        pltpu.VMEM((partners + 3, 8, 128), f32),
        dma((5,)), dma((6,)), dma((6,)), dma((4,)), dma((4,)), dma((4,)), dma((4,)),
        dma((partners,)), dma((partners,)),
    ]
    return pl.pallas_call(
        functools.partial(kernel, gx_size, gy_size),
        out_shape=(
            jax.ShapeDtypeStruct(b.shape, f32),
            jax.ShapeDtypeStruct(b.shape[1:], f32),
        ),
        in_specs=[hbm] * 5 + [smem] * 3,
        out_specs=(vmem, vmem),
        scratch_shapes=scratch,
        compiler_params=pltpu.CompilerParams(
            collective_id=0, has_side_effects=True, vmem_limit_bytes=48 * 1024 * 1024
        ),
        name="adjoint",
    )(*args)


def solution(mesh):
    in_specs = (
        P(None, "gx", "gy", None),
        P("gx", "gy", None),
        P("gx", "gy", None),
        P("gx", "gy", None),
        P("gx", "gy", None),
        P(),
        P(),
        P(),
    )
    out_specs = (P(None, "gx", "gy", None), P("gx", "gy", None))
    return jax.shard_map(
        per_device, mesh=mesh, in_specs=in_specs, out_specs=out_specs, check_vma=False
    )
```

```python
import functools

import jax
import jax.numpy as jnp
from jax import lax
from jax.experimental import pallas as pl
from jax.experimental.pallas import tpu as pltpu
from jax.sharding import PartitionSpec as P

MESH = pl.DeviceIdType.MESH
RING_X = 4


def pick(table, label):
    low = jnp.where(label == 0, table[0], table[1])
    high = jnp.where(label == 2, table[2], table[3])
    return jnp.where(label < 2, low, high)


def fold(plane):
    rows, lanes = plane.shape
    total = None
    for i in range(0, rows, 8):
        for j in range(0, lanes, 128):
            part = plane[i : i + 8, j : j + 128]
            total = part if total is None else total + part
    return total


def kernel(
    gx_size, gy_size,
    b_hbm, warm_hbm, yield_hbm, print_hbm, label_hbm, rigidity_hbm, dilatation_hbm, diffusivity_hbm,
    U, T, coef_out,
    B, H, WARM, YIELD, PRINT, LABEL, TS, WY, WZ, D, S3,
    y1_lo, y1_hi, ry1_lo, ry1_hi, rx1_lo, rx1_hi,
    y2_lo, y2_hi, ry2_lo, ry2_hi, rx2_lo, rx2_hi,
    y3_lo, y3_hi, ry3_lo, ry3_hi, rx3_lo, rx3_hi,
    sums,
    rigidity, dilatation, diffusivity,
    load_sem, send1, recv1, send2, recv2, send3, recv3, send_r, recv_r,
):
    _, nx, ny, nz = b_hbm.shape
    gx, gy = lax.axis_index("gx"), lax.axis_index("gy")
    ring_z = gy_size // RING_X
    gz, gq = gy // RING_X, gy % RING_X
    up_x, down_x = (gx + 1) % gx_size, (gx + gx_size - 1) % gx_size
    up_y, down_y = (gy + 1) % gy_size, (gy + gy_size - 1) % gy_size
    has_lo_x, has_hi_x = gx > 0, gx < gx_size - 1
    has_lo_y, has_hi_y = gy > 0, gy < gy_size - 1
    stages = []
    for stage, count in enumerate((gx_size, ring_z, RING_X)):
        partners = []
        for k in range(1, count):
            if stage == 0:
                partners.append(((gx + k) % gx_size, gy))
            elif stage == 1:
                partners.append((gx, ((gz + k) % ring_z) * RING_X + gq))
            else:
                partners.append((gx, gz * RING_X + (gq + k) % RING_X))
        stages.append(partners)

    loads = [
        pltpu.make_async_copy(rigidity_hbm, rigidity, load_sem.at[5]),
        pltpu.make_async_copy(dilatation_hbm, dilatation, load_sem.at[6]),
        pltpu.make_async_copy(diffusivity_hbm, diffusivity, load_sem.at[7]),
        pltpu.make_async_copy(label_hbm, LABEL, load_sem.at[0]),
        pltpu.make_async_copy(yield_hbm, YIELD, load_sem.at[1]),
        pltpu.make_async_copy(print_hbm, PRINT, load_sem.at[2]),
        pltpu.make_async_copy(warm_hbm, WARM, load_sem.at[3]),
        pltpu.make_async_copy(b_hbm, B, load_sem.at[4]),
    ]
    for load in loads:
        load.start()

    barrier = pltpu.get_barrier_semaphore()
    greeted = [(up_x, gy), (down_x, gy), (gx, up_y), (gx, down_y)]
    for partners in stages:
        greeted += partners
    for partner in greeted:
        pl.semaphore_signal(barrier, inc=1, device_id=partner, device_id_type=MESH)

    for inside, halos in (
        (has_lo_x, (rx1_lo, rx2_lo, rx3_lo)),
        (has_hi_x, (rx1_hi, rx2_hi, rx3_hi)),
        (has_lo_y, (ry1_lo, ry2_lo, ry3_lo)),
        (has_hi_y, (ry1_hi, ry2_hi, ry3_hi)),
    ):
        @pl.when(jnp.logical_not(inside))
        def _():
            for halo in halos:
                halo[...] = jnp.zeros(halo.shape, jnp.float32)

    row = lax.broadcasted_iota(jnp.int32, (ny, nz), 0)
    lane = lax.broadcasted_iota(jnp.int32, (ny, nz), 1)
    first_row, last_row = row == 0, row == ny - 1
    last_lane = lane == nz - 1
    edge_lane = (lane == 0) | last_lane

    def remote(src, dst, send, recv, partner):
        return pltpu.make_async_remote_copy(
            src_ref=src, dst_ref=dst, send_sem=send, recv_sem=recv,
            device_id=partner, device_id_type=MESH,
        )

    def start_faces(up, down, has_lo, has_hi):
        @pl.when(has_hi)
        def _():
            for copy in up:
                copy.start()

        @pl.when(has_lo)
        def _():
            for copy in down:
                copy.start()

    def finish_faces(up, down, has_lo, has_hi):
        @pl.when(has_hi)
        def _():
            for copy in up:
                copy.wait_send()
            for copy in down:
                copy.wait_recv()

        @pl.when(has_lo)
        def _():
            for copy in down:
                copy.wait_send()
            for copy in up:
                copy.wait_recv()

    def faces_y(ylo, yhi, rlo, rhi, send, recv):
        return (
            [remote(yhi, rlo, send.at[0], recv.at[0], (gx, up_y))],
            [remote(ylo, rhi, send.at[1], recv.at[1], (gx, down_y))],
            has_lo_y, has_hi_y,
        )

    def faces_x(field, rlo, rhi, send, recv):
        return (
            [remote(field.at[:, nx - 1], rlo, send.at[2], recv.at[2], (up_x, gy))],
            [remote(field.at[:, 0], rhi, send.at[3], recv.at[3], (down_x, gy))],
            has_lo_x, has_hi_x,
        )

    for load in loads:
        load.wait()

    def properties(x, carry):
        label = LABEL[x]
        stiffness = (
            pick(rigidity, label)
            * (1.0 - 0.7 * YIELD[x].astype(jnp.float32))
            * (0.05 + 0.95 * PRINT[x].astype(jnp.float32))
        )
        half = 0.5 * stiffness
        H[x] = half
        TS[x] = pick(dilatation, label) * (0.5 + WARM[x]) * half
        half_c = 0.5 * pick(diffusivity, label)
        S3[2, x] = half_c
        at = pl.ds(x, 1)
        for c in range(3):
            y1_lo[c, at, :] = B[c, x, 0:1, :]
            y1_hi[c, at, :] = B[c, x, ny - 1 : ny, :]
        y1_lo[3, at, :] = half[0:1, :]
        y1_hi[3, at, :] = half[ny - 1 : ny, :]
        y3_lo[2, at, :] = half_c[0:1, :]
        y3_hi[2, at, :] = half_c[ny - 1 : ny, :]
        return carry

    lax.fori_loop(0, nx, properties, 0)

    pl.semaphore_wait(barrier, len(greeted))

    copies1y = faces_y(y1_lo, y1_hi, ry1_lo, ry1_hi, send1, recv1)
    fields = pl.ds(0, 3)
    copies1x = (
        [
            remote(B.at[:, nx - 1], rx1_lo.at[fields], send1.at[2], recv1.at[2], (up_x, gy)),
            remote(H.at[nx - 1], rx1_lo.at[3], send1.at[4], recv1.at[4], (up_x, gy)),
        ],
        [
            remote(B.at[:, 0], rx1_hi.at[fields], send1.at[3], recv1.at[3], (down_x, gy)),
            remote(H.at[0], rx1_hi.at[3], send1.at[5], recv1.at[5], (down_x, gy)),
        ],
        has_lo_x, has_hi_x,
    )
    start_faces(*copies1y)
    start_faces(*copies1x)

    def next_y(plane):
        return pltpu.roll(plane, ny - 1, 0)

    def prev_y(plane):
        return pltpu.roll(plane, 1, 0)

    def next_z(plane):
        return pltpu.roll(plane, nz - 1, 1)

    def prev_z(plane):
        return pltpu.roll(plane, 1, 1)

    def inflow(field, c, x, here, wxm, wxp, wy, wz):
        total = wxp * (field[c, jnp.minimum(x + 1, nx - 1)] - here)
        total += wxm * (field[c, jnp.maximum(x - 1, 0)] - here)
        flux = wy * (next_y(here) - here)
        total += flux - prev_y(flux)
        flux = wz * (next_z(here) - here)
        return total + (flux - prev_z(flux))

    def weights_yz(half):
        wy = jnp.where(last_row, 0.0, half + next_y(half))
        wz = jnp.where(last_lane, 0.0, half + next_z(half))
        return wy, wz

    def weights_x(x, half):
        return half + H[jnp.maximum(x - 1, 0)], half + H[jnp.minimum(x + 1, nx - 1)]

    zero = jnp.zeros((8, 128), jnp.float32)

    def first_image(x, carry):
        bu, uu = carry
        at = pl.ds(x, 1)
        half = H[x]
        wxm, wxp = weights_x(x, half)
        wy, wz = weights_yz(half)
        diag = 0.5 + jnp.where(edge_lane, half, 0.0)
        WY[x], WZ[x], D[x] = wy, wz, diag
        for c in range(3):
            here = B[c, x]
            image = diag * here - inflow(B, c, x, here, wxm, wxp, wy, wz)
            U[c, x] = image
            y2_lo[c, at, :] = image[0:1, :]
            y2_hi[c, at, :] = image[ny - 1 : ny, :]
            bu += fold(here * image)
            uu += fold(image * image)
        return bu, uu

    bu, uu = lax.fori_loop(0, nx, first_image, (zero, zero))

    finish_faces(*copies1x)
    for x, halo in ((0, rx1_lo), (nx - 1, rx1_hi)):
        weight = H[x] + halo[3]
        for c in range(3):
            here, image = B[c, x], U[c, x]
            more = weight * (here - halo[c])
            bu += fold(here * more)
            uu += fold(more * (2.0 * image + more))
            image += more
            U[c, x] = image
            y2_lo[c, x : x + 1, :] = image[0:1, :]
            y2_hi[c, x : x + 1, :] = image[ny - 1 : ny, :]
    finish_faces(*copies1y)
    for face, image, halo in ((y1_lo, y2_lo, ry1_lo), (y1_hi, y2_hi, ry1_hi)):
        weight = face[3] + halo[3]
        for c in range(3):
            more = weight * (face[c] - halo[c])
            bu += fold(face[c] * more)
            uu += fold(more * (2.0 * image[c] + more))
            image[c] = image[c] + more

    copies2y = faces_y(y2_lo, y2_hi, ry2_lo, ry2_hi, send2, recv2)
    start_faces(*copies2y)

    def set_rows(x, carry):
        at = pl.ds(x, 1)
        for c in range(3):
            U[c, x, 0:1, :] = y2_lo[c, at, :]
            U[c, x, ny - 1 : ny, :] = y2_hi[c, at, :]
        return carry

    lax.fori_loop(0, nx, set_rows, 0)
    copies2x = faces_x(U, rx2_lo, rx2_hi, send2, recv2)
    start_faces(*copies2x)

    def everywhere(tile):
        total = jnp.sum(jnp.sum(tile, axis=0, keepdims=True), axis=1, keepdims=True)
        return jnp.broadcast_to(total, (1, 128))

    weight = everywhere(uu)
    sigma = everywhere(bu) / jnp.where(weight > 0.0, weight, 1.0)
    sigma_all = jnp.broadcast_to(sigma[:, 0:1], (ny, nz))

    def second_image(x, carry):
        uu, rr, ru, rv, uv = carry
        half = H[x]
        wxm, wxp = weights_x(x, half)
        wy, wz, diag = WY[x], WZ[x], D[x]
        for c in range(3):
            here = U[c, x]
            image = diag * here - inflow(U, c, x, here, wxm, wxp, wy, wz)
            rest = B[c, x] - sigma_all * here
            uu += fold(here * here)
            rr += fold(rest * rest)
            ru += fold(rest * here)
            rv += fold(rest * image)
            uv += fold(here * image)
        return uu, rr, ru, rv, uv

    uu, rr, ru, rv, uv = lax.fori_loop(0, nx, second_image, (zero,) * 5)

    def source_of(field, xlo, xhi, rlo, rhi, out, ylo, yhi):
        def body(x, below, above):
            at = pl.ds(x, 1)
            mid, last = field[1, x], field[2, x]
            div = above - below
            div += jnp.where(last_row, rhi[1, at, :], next_y(mid))
            div -= jnp.where(first_row, rlo[1, at, :], prev_y(mid))
            div += jnp.where(last_lane, 0.0, next_z(last)) - jnp.where(lane == 0, 0.0, prev_z(last))
            source = -TS[x] * div
            S3[out, x] = source
            ylo[out, at, :] = source[0:1, :]
            yhi[out, at, :] = source[ny - 1 : ny, :]

        def inner(x, carry):
            body(x, field[0, x - 1], field[0, x + 1])
            return carry

        body(0, xlo[0], field[0, 1])
        lax.fori_loop(1, nx - 1, inner, 0)
        body(nx - 1, field[0, nx - 2], xhi[0])

    source_of(B, rx1_lo, rx1_hi, ry1_lo, ry1_hi, 0, y3_lo, y3_hi)

    finish_faces(*copies2x)
    for x, halo, stiff in ((0, rx2_lo, rx1_lo), (nx - 1, rx2_hi, rx1_hi)):
        weight = H[x] + stiff[3]
        for c in range(3):
            here = U[c, x]
            more = weight * (here - halo[c])
            rv += fold((B[c, x] - sigma_all * here) * more)
            uv += fold(here * more)
    finish_faces(*copies2y)
    sigma_face = jnp.broadcast_to(sigma[:, 0:1], (nx, nz))
    for face, image, halo, stiff in ((y1_lo, y2_lo, ry2_lo, ry1_lo), (y1_hi, y2_hi, ry2_hi, ry1_hi)):
        weight = face[3] + stiff[3]
        for c in range(3):
            here = image[c]
            more = weight * (here - halo[c])
            rv += fold((face[c] - sigma_face * here) * more)
            uv += fold(here * more)

    def lanes(tile):
        return jnp.sum(tile, axis=0, keepdims=True)

    def pack(parts):
        index = lax.broadcasted_iota(jnp.int32, (8, 128), 0)
        tile = jnp.zeros((8, 128), jnp.float32)
        for i, part in enumerate(parts):
            tile = jnp.where(index == i, jnp.broadcast_to(part, (8, 128)), tile)
        return tile

    def merge(tiles):
        rows = [[tile[i : i + 1, :] for i in range(7)] for tile in tiles]
        weight = sum(r[6] for r in rows)
        sigma = sum(r[6] * r[5] for r in rows) / jnp.where(weight > 0.0, weight, 1.0)
        out = [0.0] * 5
        for uu, rr, ru, rv, uv, own, _ in rows:
            tau = own - sigma
            shifted = (
                uu, rr + tau * (2.0 * ru + tau * uu), ru + tau * uu, rv + tau * uv, uv,
            )
            out = [a + b for a, b in zip(out, shifted)]
        return out + [sigma, weight]

    weight = everywhere(uu)
    state = [lanes(m) for m in (uu, rr, ru, rv, uv)] + [sigma, weight]

    def reduce_start(stage, state):
        base = sum(len(s) for s in stages[:stage])
        own = sums.at[base + stage]
        sums[base + stage] = pack(state)
        copies = []
        for k, partner in enumerate(stages[stage]):
            copies.append(
                remote(own, sums.at[base + stage + 1 + k], send_r.at[base + k], recv_r.at[base + k], partner)
            )
        for copy in copies:
            copy.start()
        return copies

    def reduce_finish(stage, copies):
        base = sum(len(s) for s in stages[:stage]) + stage
        for copy in copies:
            copy.wait()
        return merge([sums[base + k] for k in range(len(copies) + 1)])

    pending = reduce_start(0, state)
    source_of(U, rx2_lo, rx2_hi, ry2_lo, ry2_hi, 1, y3_lo, y3_hi)
    copies3y = faces_y(y3_lo, y3_hi, ry3_lo, ry3_hi, send3, recv3)
    copies3x = faces_x(S3, rx3_lo, rx3_hi, send3, recv3)
    start_faces(*copies3y)
    start_faces(*copies3x)
    state = reduce_finish(0, pending)
    pending = reduce_start(1, state)

    def conduct(x, carry):
        half = S3[2, x]
        wxm = half + S3[2, jnp.maximum(x - 1, 0)]
        wxp = half + S3[2, jnp.minimum(x + 1, nx - 1)]
        wy, wz = weights_yz(half)
        diag = 1.0 - 0.15 * jnp.where(edge_lane, half, 0.0)
        for c in range(2):
            here = S3[c, x]
            T[c, x] = diag * here + 0.15 * inflow(S3, c, x, here, wxm, wxp, wy, wz)
        return carry

    lax.fori_loop(0, nx, conduct, 0)
    state = reduce_finish(1, pending)
    pending = reduce_start(2, state)

    finish_faces(*copies3x)
    for x, halo in ((0, rx3_lo), (nx - 1, rx3_hi)):
        weight = 0.15 * (S3[2, x] + halo[2])
        for c in range(2):
            T[c, x] = T[c, x] + weight * (halo[c] - S3[c, x])
    finish_faces(*copies3y)
    for face, halo in ((y3_lo, ry3_lo), (y3_hi, ry3_hi)):
        weight = 0.15 * (face[2] + halo[2])
        for c in range(2):
            halo[c] = weight * (halo[c] - face[c])

    def add_rows(x, carry):
        at = pl.ds(x, 1)
        for c in range(2):
            T[c, x, 0:1, :] = T[c, x, 0:1, :] + ry3_lo[c, at, :]
            T[c, x, ny - 1 : ny, :] = T[c, x, ny - 1 : ny, :] + ry3_hi[c, at, :]
        return carry

    lax.fori_loop(0, nx, add_rows, 0)
    state = reduce_finish(2, pending)

    uu, rr, ru, rv, uv, sigma = [
        jnp.sum(part, axis=1, keepdims=True) for part in state[:5]
    ] + [state[5][:, 0:1]]
    energy = ru + sigma * uu
    norm = rr + sigma * (2.0 * ru + sigma * uu)
    step0 = norm / energy
    tau = sigma - step0
    norm1 = rr + tau * (2.0 * ru + tau * uu)
    ru, rv = ru + tau * uu, rv + tau * uv
    ratio = norm1 / norm
    curve = (ru - step0 * rv) + ratio * (2.0 * ru + ratio * energy)
    step1 = norm1 / curve
    coef_out[0:1, :] = jnp.broadcast_to(step0 + step1 * (1.0 + ratio), (1, 128))
    coef_out[1:2, :] = jnp.broadcast_to(-step1 * step0, (1, 128))


def combine(coef, b, u, t, x_out, th_out):
    coef_b = jnp.broadcast_to(coef[0:1, 0:1], x_out.shape[2:])
    coef_u = jnp.broadcast_to(coef[1:2, 0:1], x_out.shape[2:])
    for x in range(th_out.shape[0]):
        for c in range(3):
            x_out[c, x] = coef_b * b[c, x] + coef_u * u[c, x]
        th_out[x] = coef_b * t[0, x] + coef_u * t[1, x]


def per_device(*args):
    b = args[0]
    _, nx, ny, nz = b.shape
    gx_size, gy_size = lax.axis_size("gx"), lax.axis_size("gy")
    partners = gx_size - 1 + gy_size // RING_X - 1 + RING_X - 1
    f32 = jnp.float32
    block = (nx, ny, nz)
    hbm, vmem = (pl.BlockSpec(memory_space=m) for m in (pltpu.HBM, pltpu.VMEM))
    dma = pltpu.SemaphoreType.DMA
    scratch = [pltpu.VMEM((3,) + block, f32)]
    scratch += [pltpu.VMEM(block, t) for t in [f32] * 2 + [jnp.int32] * 3 + [f32] * 4]
    scratch += [pltpu.VMEM((3,) + block, f32)]
    for fields in (4, 3, 3):
        scratch += [pltpu.VMEM((fields, nx, nz), f32)] * 4
        scratch += [pltpu.VMEM((fields, ny, nz), f32)] * 2
    scratch += [pltpu.VMEM((partners + 3, 8, 128), f32)]
    scratch += [pltpu.SMEM((4,), f32)] * 3
    scratch += [dma((8,))] + [dma((6,))] * 2 + [dma((4,))] * 4 + [dma((partners,))] * 2
    u, t, coef = pl.pallas_call(
        functools.partial(kernel, gx_size, gy_size),
        out_shape=(
            jax.ShapeDtypeStruct((3,) + block, f32),
            jax.ShapeDtypeStruct((2,) + block, f32),
            jax.ShapeDtypeStruct((8, 128), f32),
        ),
        in_specs=[hbm] * 8,
        out_specs=(vmem, vmem, vmem),
        scratch_shapes=scratch,
        compiler_params=pltpu.CompilerParams(
            collective_id=0, has_side_effects=True, vmem_limit_bytes=40 * 1024 * 1024
        ),
        name="adjoint",
    )(*[pltpu.with_memory_space_constraint(arg, pltpu.HBM) for arg in args])
    return pl.pallas_call(
        combine,
        grid=(4,),
        out_shape=(
            jax.ShapeDtypeStruct((3,) + block, f32), jax.ShapeDtypeStruct(block, f32),
        ),
        in_specs=[
            pl.BlockSpec((8, 128), lambda i: (0, 0)),
            pl.BlockSpec((3, nx // 4, ny, nz), lambda i: (0, i, 0, 0)),
            pl.BlockSpec((3, nx // 4, ny, nz), lambda i: (0, i, 0, 0)),
            pl.BlockSpec((2, nx // 4, ny, nz), lambda i: (0, i, 0, 0)),
        ],
        out_specs=(
            pl.BlockSpec((3, nx // 4, ny, nz), lambda i: (0, i, 0, 0)),
            pl.BlockSpec((nx // 4, ny, nz), lambda i: (i, 0, 0)),
        ),
        compiler_params=pltpu.CompilerParams(vmem_limit_bytes=24 * 1024 * 1024),
        name="combine",
    )(coef, b, u, t)


def solution(mesh):
    in_specs = (
        P(None, "gx", "gy", None),
        P("gx", "gy", None),
        P("gx", "gy", None),
        P("gx", "gy", None),
        P("gx", "gy", None),
        P(),
        P(),
        P(),
    )
    out_specs = (P(None, "gx", "gy", None), P("gx", "gy", None))
    return jax.shard_map(
        per_device, mesh=mesh, in_specs=in_specs, out_specs=out_specs, check_vma=False
    )
```

```python
import functools
import itertools

import jax
import jax.numpy as jnp
from jax import lax
from jax.experimental import pallas as pl
from jax.experimental.pallas import tpu as pltpu
from jax.sharding import PartitionSpec as P

MESH = pl.DeviceIdType.MESH
RING_X = 4


def pick(table, label):
    low = jnp.where(label == 0, table[0], table[1])
    high = jnp.where(label == 2, table[2], table[3])
    return jnp.where(label < 2, low, high)


def fold(plane):
    rows, lanes = plane.shape
    total = None
    for i in range(0, rows, 8):
        for j in range(0, lanes, 128):
            part = plane[i : i + 8, j : j + 128]
            total = part if total is None else total + part
    return total


GROUPS = ("cz", "xy")
PIECES = 2


def offset_partners(group, gx, gy, gx_size, gy_size):
    sizes = {"c": 2, "y": gx_size // 2, "z": gy_size // RING_X, "x": RING_X}
    place = {"c": gx % 2, "y": gx // 2, "z": gy // RING_X, "x": gy % RING_X}
    partners = []

    def hops(offsets):
        return sum(min(o, sizes[axis] - o) for axis, o in zip(group, offsets))

    every = itertools.product(*[range(sizes[axis]) for axis in group])
    for offsets in sorted(every, key=hops, reverse=True):
        if any(offsets):
            to = dict(place)
            for axis, offset in zip(group, offsets):
                to[axis] = (place[axis] + offset) % sizes[axis]
            partners.append((to["y"] * 2 + to["c"], to["z"] * RING_X + to["x"]))
    return partners


def kernel(
    gx_size, gy_size,
    b_hbm, warm_hbm, yield_hbm, print_hbm, label_hbm, rigidity_hbm, dilatation_hbm, diffusivity_hbm,
    U, T, coef_out,
    B, H, WARM, YIELD, PRINT, LABEL, TS, WY, WZ, D, S3,
    y1_lo, y1_hi, ry1_lo, ry1_hi, rx1_lo, rx1_hi,
    y2_lo, y2_hi, ry2_lo, ry2_hi, rx2_lo, rx2_hi,
    y3_lo, y3_hi, ry3_lo, ry3_hi, rx3_lo, rx3_hi,
    sums,
    rigidity, dilatation, diffusivity,
    load_sem, send1, recv1, send2, recv2, send3, recv3, send_r, recv_r,
):
    _, nx, ny, nz = b_hbm.shape
    gx, gy = lax.axis_index("gx"), lax.axis_index("gy")
    ring_z = gy_size // RING_X
    gz, gq = gy // RING_X, gy % RING_X
    up_x, down_x = (gx + 1) % gx_size, (gx + gx_size - 1) % gx_size
    up_y, down_y = (gy + 1) % gy_size, (gy + gy_size - 1) % gy_size
    has_lo_x, has_hi_x = gx > 0, gx < gx_size - 1
    has_lo_y, has_hi_y = gy > 0, gy < gy_size - 1
    stages = [offset_partners(group, gx, gy, gx_size, gy_size) for group in GROUPS]

    loads = [
        pltpu.make_async_copy(rigidity_hbm, rigidity, load_sem.at[5]),
        pltpu.make_async_copy(dilatation_hbm, dilatation, load_sem.at[6]),
        pltpu.make_async_copy(diffusivity_hbm, diffusivity, load_sem.at[7]),
        pltpu.make_async_copy(label_hbm, LABEL, load_sem.at[0]),
        pltpu.make_async_copy(yield_hbm, YIELD, load_sem.at[1]),
        pltpu.make_async_copy(print_hbm, PRINT, load_sem.at[2]),
        pltpu.make_async_copy(warm_hbm, WARM, load_sem.at[3]),
        pltpu.make_async_copy(b_hbm, B, load_sem.at[4]),
    ]
    for load in loads:
        load.start()

    barrier = pltpu.get_barrier_semaphore()
    greeted = [(up_x, gy), (down_x, gy), (gx, up_y), (gx, down_y)]
    for partners in stages:
        greeted += partners
    for partner in greeted:
        pl.semaphore_signal(barrier, inc=1, device_id=partner, device_id_type=MESH)

    for inside, halos in (
        (has_lo_x, (rx1_lo, rx2_lo, rx3_lo)),
        (has_hi_x, (rx1_hi, rx2_hi, rx3_hi)),
        (has_lo_y, (ry1_lo, ry2_lo, ry3_lo)),
        (has_hi_y, (ry1_hi, ry2_hi, ry3_hi)),
    ):
        @pl.when(jnp.logical_not(inside))
        def _():
            for halo in halos:
                halo[...] = jnp.zeros(halo.shape, jnp.float32)

    row = lax.broadcasted_iota(jnp.int32, (ny, nz), 0)
    lane = lax.broadcasted_iota(jnp.int32, (ny, nz), 1)
    first_row, last_row = row == 0, row == ny - 1
    last_lane = lane == nz - 1
    edge_lane = (lane == 0) | last_lane

    def remote(src, dst, send, recv, partner):
        return pltpu.make_async_remote_copy(
            src_ref=src, dst_ref=dst, send_sem=send, recv_sem=recv,
            device_id=partner, device_id_type=MESH,
        )

    def start_faces(up, down, has_lo, has_hi):
        @pl.when(has_hi)
        def _():
            for copy in up:
                copy.start()

        @pl.when(has_lo)
        def _():
            for copy in down:
                copy.start()

    def finish_faces(up, down, has_lo, has_hi):
        @pl.when(has_hi)
        def _():
            for copy in up:
                copy.wait_send()
            for copy in down:
                copy.wait_recv()

        @pl.when(has_lo)
        def _():
            for copy in down:
                copy.wait_send()
            for copy in up:
                copy.wait_recv()

    def faces_y(ylo, yhi, rlo, rhi, send, recv):
        return (
            [remote(yhi, rlo, send.at[0], recv.at[0], (gx, up_y))],
            [remote(ylo, rhi, send.at[1], recv.at[1], (gx, down_y))],
            has_lo_y, has_hi_y,
        )

    def faces_x(field, rlo, rhi, send, recv):
        return (
            [remote(field.at[:, nx - 1], rlo, send.at[2], recv.at[2], (up_x, gy))],
            [remote(field.at[:, 0], rhi, send.at[3], recv.at[3], (down_x, gy))],
            has_lo_x, has_hi_x,
        )

    for load in loads:
        load.wait()

    def properties(x, carry):
        label = LABEL[x]
        stiffness = (
            pick(rigidity, label)
            * (1.0 - 0.7 * YIELD[x].astype(jnp.float32))
            * (0.05 + 0.95 * PRINT[x].astype(jnp.float32))
        )
        half = 0.5 * stiffness
        H[x] = half
        TS[x] = pick(dilatation, label) * (0.5 + WARM[x]) * half
        half_c = 0.5 * pick(diffusivity, label)
        S3[2, x] = half_c
        at = pl.ds(x, 1)
        for c in range(3):
            y1_lo[c, at, :] = B[c, x, 0:1, :]
            y1_hi[c, at, :] = B[c, x, ny - 1 : ny, :]
        y1_lo[3, at, :] = half[0:1, :]
        y1_hi[3, at, :] = half[ny - 1 : ny, :]
        y3_lo[2, at, :] = half_c[0:1, :]
        y3_hi[2, at, :] = half_c[ny - 1 : ny, :]
        return carry

    lax.fori_loop(0, nx, properties, 0)

    pl.semaphore_wait(barrier, len(greeted))

    copies1y = faces_y(y1_lo, y1_hi, ry1_lo, ry1_hi, send1, recv1)
    fields = pl.ds(0, 3)
    copies1x = (
        [
            remote(B.at[:, nx - 1], rx1_lo.at[fields], send1.at[2], recv1.at[2], (up_x, gy)),
            remote(H.at[nx - 1], rx1_lo.at[3], send1.at[4], recv1.at[4], (up_x, gy)),
        ],
        [
            remote(B.at[:, 0], rx1_hi.at[fields], send1.at[3], recv1.at[3], (down_x, gy)),
            remote(H.at[0], rx1_hi.at[3], send1.at[5], recv1.at[5], (down_x, gy)),
        ],
        has_lo_x, has_hi_x,
    )
    start_faces(*copies1y)
    start_faces(*copies1x)

    def next_y(plane):
        return pltpu.roll(plane, ny - 1, 0)

    def prev_y(plane):
        return pltpu.roll(plane, 1, 0)

    def next_z(plane):
        return pltpu.roll(plane, nz - 1, 1)

    def prev_z(plane):
        return pltpu.roll(plane, 1, 1)

    def inflow(field, c, x, here, wxm, wxp, wy, wz):
        total = wxp * (field[c, jnp.minimum(x + 1, nx - 1)] - here)
        total += wxm * (field[c, jnp.maximum(x - 1, 0)] - here)
        flux = wy * (next_y(here) - here)
        total += flux - prev_y(flux)
        flux = wz * (next_z(here) - here)
        return total + (flux - prev_z(flux))

    def weights_yz(half):
        wy = jnp.where(last_row, 0.0, half + next_y(half))
        wz = jnp.where(last_lane, 0.0, half + next_z(half))
        return wy, wz

    def weights_x(x, half):
        return half + H[jnp.maximum(x - 1, 0)], half + H[jnp.minimum(x + 1, nx - 1)]

    zero = jnp.zeros((8, 128), jnp.float32)

    def first_image(x, carry):
        bu, uu = carry
        at = pl.ds(x, 1)
        half = H[x]
        wxm, wxp = weights_x(x, half)
        wy, wz = weights_yz(half)
        diag = 0.5 + jnp.where(edge_lane, half, 0.0)
        WY[x], WZ[x], D[x] = wy, wz, diag
        for c in range(3):
            here = B[c, x]
            image = diag * here - inflow(B, c, x, here, wxm, wxp, wy, wz)
            U[c, x] = image
            y2_lo[c, at, :] = image[0:1, :]
            y2_hi[c, at, :] = image[ny - 1 : ny, :]
            bu += fold(here * image)
            uu += fold(image * image)
        return bu, uu

    bu, uu = lax.fori_loop(0, nx, first_image, (zero, zero))

    finish_faces(*copies1x)
    for x, halo in ((0, rx1_lo), (nx - 1, rx1_hi)):
        weight = H[x] + halo[3]
        for c in range(3):
            here, image = B[c, x], U[c, x]
            more = weight * (here - halo[c])
            bu += fold(here * more)
            uu += fold(more * (2.0 * image + more))
            image += more
            U[c, x] = image
            y2_lo[c, x : x + 1, :] = image[0:1, :]
            y2_hi[c, x : x + 1, :] = image[ny - 1 : ny, :]
    finish_faces(*copies1y)
    for face, image, halo in ((y1_lo, y2_lo, ry1_lo), (y1_hi, y2_hi, ry1_hi)):
        weight = face[3] + halo[3]
        for c in range(3):
            more = weight * (face[c] - halo[c])
            bu += fold(face[c] * more)
            uu += fold(more * (2.0 * image[c] + more))
            image[c] = image[c] + more

    copies2y = faces_y(y2_lo, y2_hi, ry2_lo, ry2_hi, send2, recv2)
    start_faces(*copies2y)

    def set_rows(x, carry):
        at = pl.ds(x, 1)
        for c in range(3):
            U[c, x, 0:1, :] = y2_lo[c, at, :]
            U[c, x, ny - 1 : ny, :] = y2_hi[c, at, :]
        return carry

    lax.fori_loop(0, nx, set_rows, 0)
    copies2x = faces_x(U, rx2_lo, rx2_hi, send2, recv2)
    start_faces(*copies2x)

    def everywhere(tile):
        total = jnp.sum(jnp.sum(tile, axis=0, keepdims=True), axis=1, keepdims=True)
        return jnp.broadcast_to(total, (1, 128))

    weight = everywhere(uu)
    sigma = everywhere(bu) / jnp.where(weight > 0.0, weight, 1.0)
    sigma_all = jnp.broadcast_to(sigma[:, 0:1], (ny, nz))

    def second_image(x, carry):
        uu, rr, ru, rv, uv = carry
        half = H[x]
        wxm, wxp = weights_x(x, half)
        wy, wz, diag = WY[x], WZ[x], D[x]
        for c in range(3):
            here = U[c, x]
            image = diag * here - inflow(U, c, x, here, wxm, wxp, wy, wz)
            rest = B[c, x] - sigma_all * here
            uu += fold(here * here)
            rr += fold(rest * rest)
            ru += fold(rest * here)
            rv += fold(rest * image)
            uv += fold(here * image)
        return uu, rr, ru, rv, uv

    uu, rr, ru, rv, uv = lax.fori_loop(0, nx, second_image, (zero,) * 5)

    def source_of(field, xlo, xhi, rlo, rhi, out, ylo, yhi):
        def body(x, below, above):
            at = pl.ds(x, 1)
            mid, last = field[1, x], field[2, x]
            div = above - below
            div += jnp.where(last_row, rhi[1, at, :], next_y(mid))
            div -= jnp.where(first_row, rlo[1, at, :], prev_y(mid))
            div += jnp.where(last_lane, 0.0, next_z(last)) - jnp.where(lane == 0, 0.0, prev_z(last))
            source = -TS[x] * div
            S3[out, x] = source
            ylo[out, at, :] = source[0:1, :]
            yhi[out, at, :] = source[ny - 1 : ny, :]

        def inner(x, carry):
            body(x, field[0, x - 1], field[0, x + 1])
            return carry

        body(0, xlo[0], field[0, 1])
        lax.fori_loop(1, nx - 1, inner, 0)
        body(nx - 1, field[0, nx - 2], xhi[0])

    source_of(B, rx1_lo, rx1_hi, ry1_lo, ry1_hi, 0, y3_lo, y3_hi)

    finish_faces(*copies2x)
    for x, halo, stiff in ((0, rx2_lo, rx1_lo), (nx - 1, rx2_hi, rx1_hi)):
        weight = H[x] + stiff[3]
        for c in range(3):
            here = U[c, x]
            more = weight * (here - halo[c])
            rv += fold((B[c, x] - sigma_all * here) * more)
            uv += fold(here * more)
    finish_faces(*copies2y)
    sigma_face = jnp.broadcast_to(sigma[:, 0:1], (nx, nz))
    for face, image, halo, stiff in ((y1_lo, y2_lo, ry2_lo, ry1_lo), (y1_hi, y2_hi, ry2_hi, ry1_hi)):
        weight = face[3] + stiff[3]
        for c in range(3):
            here = image[c]
            more = weight * (here - halo[c])
            rv += fold((face[c] - sigma_face * here) * more)
            uv += fold(here * more)

    def lanes(tile):
        return jnp.sum(tile, axis=0, keepdims=True)

    def pack(parts):
        index = lax.broadcasted_iota(jnp.int32, (8, 128), 0)
        tile = jnp.zeros((8, 128), jnp.float32)
        for i, part in enumerate(parts):
            tile = jnp.where(index == i, jnp.broadcast_to(part, (8, 128)), tile)
        return tile

    def merge(tiles):
        rows = [[tile[i : i + 1, :] for i in range(7)] for tile in tiles]
        weight = sum(r[6] for r in rows)
        sigma = sum(r[6] * r[5] for r in rows) / jnp.where(weight > 0.0, weight, 1.0)
        out = [0.0] * 5
        for uu, rr, ru, rv, uv, own, _ in rows:
            tau = own - sigma
            shifted = (
                uu, rr + tau * (2.0 * ru + tau * uu), ru + tau * uu, rv + tau * uv, uv,
            )
            out = [a + b for a, b in zip(out, shifted)]
        return out + [sigma, weight]

    weight = everywhere(uu)
    state = [lanes(m) for m in (uu, rr, ru, rv, uv)] + [sigma, weight]

    def reduce_start(stage, state):
        base = sum(len(s) for s in stages[:stage])
        own = sums.at[base + stage]
        sums[base + stage] = pack(state)
        copies = []
        for k, partner in enumerate(stages[stage]):
            copies.append(
                remote(own, sums.at[base + stage + 1 + k], send_r.at[base + k], recv_r.at[base + k], partner)
            )
        for copy in copies:
            copy.start()
        return copies

    def reduce_finish(stage, copies):
        base = sum(len(s) for s in stages[:stage]) + stage
        for copy in copies:
            copy.wait_recv()
        return merge([sums[base + k] for k in range(len(copies) + 1)])

    pending0 = reduce_start(0, state)
    source_of(U, rx2_lo, rx2_hi, ry2_lo, ry2_hi, 1, y3_lo, y3_hi)
    copies3y = faces_y(y3_lo, y3_hi, ry3_lo, ry3_hi, send3, recv3)
    copies3x = faces_x(S3, rx3_lo, rx3_hi, send3, recv3)
    start_faces(*copies3y)
    start_faces(*copies3x)

    def conduct(x, carry):
        half = S3[2, x]
        wxm = half + S3[2, jnp.maximum(x - 1, 0)]
        wxp = half + S3[2, jnp.minimum(x + 1, nx - 1)]
        wy, wz = weights_yz(half)
        diag = 1.0 - 0.15 * jnp.where(edge_lane, half, 0.0)
        for c in range(2):
            here = S3[c, x]
            T[c, x] = diag * here + 0.15 * inflow(S3, c, x, here, wxm, wxp, wy, wz)
        return carry

    lax.fori_loop(0, nx, conduct, 0)
    state = reduce_finish(0, pending0)
    pending1 = reduce_start(1, state)

    finish_faces(*copies3x)
    for x, halo in ((0, rx3_lo), (nx - 1, rx3_hi)):
        weight = 0.15 * (S3[2, x] + halo[2])
        for c in range(2):
            T[c, x] = T[c, x] + weight * (halo[c] - S3[c, x])
    finish_faces(*copies3y)
    for face, halo in ((y3_lo, ry3_lo), (y3_hi, ry3_hi)):
        weight = 0.15 * (face[2] + halo[2])
        for c in range(2):
            halo[c] = weight * (halo[c] - face[c])

    def add_rows(x, carry):
        at = pl.ds(x, 1)
        for c in range(2):
            T[c, x, 0:1, :] = T[c, x, 0:1, :] + ry3_lo[c, at, :]
            T[c, x, ny - 1 : ny, :] = T[c, x, ny - 1 : ny, :] + ry3_hi[c, at, :]
        return carry

    lax.fori_loop(0, nx, add_rows, 0)
    for copy in pending0:
        copy.wait_send()
    state = reduce_finish(1, pending1)
    for copy in pending1:
        copy.wait_send()

    uu, rr, ru, rv, uv, sigma = [
        jnp.sum(part, axis=1, keepdims=True) for part in state[:5]
    ] + [state[5][:, 0:1]]
    energy = ru + sigma * uu
    norm = rr + sigma * (2.0 * ru + sigma * uu)
    step0 = norm / energy
    tau = sigma - step0
    norm1 = rr + tau * (2.0 * ru + tau * uu)
    ru, rv = ru + tau * uu, rv + tau * uv
    ratio = norm1 / norm
    curve = (ru - step0 * rv) + ratio * (2.0 * ru + ratio * energy)
    step1 = norm1 / curve
    coef_out[0:1, :] = jnp.broadcast_to(step0 + step1 * (1.0 + ratio), (1, 128))
    coef_out[1:2, :] = jnp.broadcast_to(-step1 * step0, (1, 128))


def combine(coef, b, u, t, x_hbm, th_hbm, x_out, th_out, sem):
    _, nx, ny, nz = b.shape
    coef_b = jnp.broadcast_to(coef[0:1, 0:1], (ny, nz))
    coef_u = jnp.broadcast_to(coef[1:2, 0:1], (ny, nz))
    copies = []
    chunk = nx // PIECES
    for piece in range(PIECES):
        for c in range(4):
            here = piece * chunk

            def one(x, carry):
                if c < 3:
                    x_out[c, x] = coef_b * b[c, x] + coef_u * u[c, x]
                else:
                    th_out[x] = coef_b * t[0, x] + coef_u * t[1, x]
                return carry

            lax.fori_loop(here, here + chunk, one, 0, unroll=True)
            planes = pl.ds(here, chunk)
            if c < 3:
                src, dst = x_out.at[c, planes], x_hbm.at[c, planes]
            else:
                src, dst = th_out.at[planes], th_hbm.at[planes]
            copies.append(pltpu.make_async_copy(src, dst, sem.at[len(copies)]))
            copies[-1].start()
    for copy in copies:
        copy.wait()


def per_device(*args):
    b = args[0]
    _, nx, ny, nz = b.shape
    gx_size, gy_size = lax.axis_size("gx"), lax.axis_size("gy")
    partners = sum(len(offset_partners(group, 0, 0, gx_size, gy_size)) for group in GROUPS)
    f32 = jnp.float32
    block = (nx, ny, nz)
    hbm, vmem = (pl.BlockSpec(memory_space=m) for m in (pltpu.HBM, pltpu.VMEM))
    dma = pltpu.SemaphoreType.DMA
    scratch = [pltpu.VMEM((3,) + block, f32)]
    scratch += [pltpu.VMEM(block, t) for t in [f32] * 2 + [jnp.int32] * 3 + [f32] * 4]
    scratch += [pltpu.VMEM((3,) + block, f32)]
    for fields in (4, 3, 3):
        scratch += [pltpu.VMEM((fields, nx, nz), f32)] * 4
        scratch += [pltpu.VMEM((fields, ny, nz), f32)] * 2
    scratch += [pltpu.VMEM((partners + len(GROUPS), 8, 128), f32)]
    scratch += [pltpu.SMEM((4,), f32)] * 3
    scratch += [dma((8,))] + [dma((6,))] * 2 + [dma((4,))] * 4 + [dma((partners,))] * 2
    u, t, coef = pl.pallas_call(
        functools.partial(kernel, gx_size, gy_size),
        out_shape=(
            jax.ShapeDtypeStruct((3,) + block, f32),
            jax.ShapeDtypeStruct((2,) + block, f32),
            jax.ShapeDtypeStruct((8, 128), f32),
        ),
        in_specs=[hbm] * 8,
        out_specs=(vmem, vmem, vmem),
        scratch_shapes=scratch,
        compiler_params=pltpu.CompilerParams(
            collective_id=0, has_side_effects=True, vmem_limit_bytes=40 * 1024 * 1024
        ),
        name="adjoint",
    )(*[pltpu.with_memory_space_constraint(arg, pltpu.HBM) for arg in args])
    return pl.pallas_call(
        combine,
        out_shape=(
            jax.ShapeDtypeStruct((3,) + block, f32), jax.ShapeDtypeStruct(block, f32),
        ),
        in_specs=[vmem] * 4,
        out_specs=(hbm, hbm),
        scratch_shapes=[
            pltpu.VMEM((3,) + block, f32), pltpu.VMEM(block, f32), dma((4 * PIECES,)),
        ],
        compiler_params=pltpu.CompilerParams(vmem_limit_bytes=16 * 1024 * 1024),
        name="combine",
    )(coef, b, u, t)


def solution(mesh):
    in_specs = (
        P(None, "gx", "gy", None),
        P("gx", "gy", None),
        P("gx", "gy", None),
        P("gx", "gy", None),
        P("gx", "gy", None),
        P(),
        P(),
        P(),
    )
    out_specs = (P(None, "gx", "gy", None), P("gx", "gy", None))
    return jax.shard_map(
        per_device, mesh=mesh, in_specs=in_specs, out_specs=out_specs, check_vma=False
    )
```

```python
import functools
import itertools

import jax
import jax.numpy as jnp
from jax import lax
from jax.experimental import pallas as pl
from jax.experimental.pallas import tpu as pltpu
from jax.sharding import PartitionSpec as P

MESH = pl.DeviceIdType.MESH
RING_X = 4


def pick(table, label):
    low = jnp.where(label == 0, table[0], table[1])
    high = jnp.where(label == 2, table[2], table[3])
    return jnp.where(label < 2, low, high)


def fold(plane):
    rows, lanes = plane.shape
    total = None
    for i in range(0, rows, 8):
        for j in range(0, lanes, 128):
            part = plane[i : i + 8, j : j + 128]
            total = part if total is None else total + part
    return total


GROUPS = ("cz", "xy")
PIECES = 2


def offset_partners(group, gx, gy, gx_size, gy_size):
    sizes = {"c": 2, "y": gx_size // 2, "z": gy_size // RING_X, "x": RING_X}
    place = {"c": gx % 2, "y": gx // 2, "z": gy // RING_X, "x": gy % RING_X}
    partners = []

    def hops(offsets):
        return sum(min(o, sizes[axis] - o) for axis, o in zip(group, offsets))

    every = itertools.product(*[range(sizes[axis]) for axis in group])
    for offsets in sorted(every, key=hops, reverse=True):
        if any(offsets):
            to = dict(place)
            for axis, offset in zip(group, offsets):
                to[axis] = (place[axis] + offset) % sizes[axis]
            partners.append((to["y"] * 2 + to["c"], to["z"] * RING_X + to["x"]))
    return partners


def kernel(
    gx_size, gy_size,
    b_hbm, warm_hbm, yield_hbm, print_hbm, label_hbm, rigidity_hbm, dilatation_hbm, diffusivity_hbm,
    U, T, coef_out,
    B, H, WARM, YIELD, PRINT, LABEL, TS, WY, WZ, D, S3,
    y1_lo, y1_hi, ry1_lo, ry1_hi, rx1_lo, rx1_hi,
    y2_lo, y2_hi, ry2_lo, ry2_hi, rx2_lo, rx2_hi, x2_lo, x2_hi, yu_lo, yu_hi,
    y3_lo, y3_hi, ry3_lo, ry3_hi, rx3_lo, rx3_hi,
    corner, rcorner, sums,
    rigidity, dilatation, diffusivity,
    load_sem, send_c, recv_c, send1, recv1, send2, recv2, send3, recv3, send_r, recv_r,
):
    _, nx, ny, nz = b_hbm.shape
    gx, gy = lax.axis_index("gx"), lax.axis_index("gy")
    ring_z = gy_size // RING_X
    gz, gq = gy // RING_X, gy % RING_X
    up_x, down_x = (gx + 1) % gx_size, (gx + gx_size - 1) % gx_size
    up_y, down_y = (gy + 1) % gy_size, (gy + gy_size - 1) % gy_size
    has_lo_x, has_hi_x = gx > 0, gx < gx_size - 1
    has_lo_y, has_hi_y = gy > 0, gy < gy_size - 1
    stages = [offset_partners(group, gx, gy, gx_size, gy_size) for group in GROUPS]

    loads = [
        pltpu.make_async_copy(rigidity_hbm, rigidity, load_sem.at[5]),
        pltpu.make_async_copy(dilatation_hbm, dilatation, load_sem.at[6]),
        pltpu.make_async_copy(diffusivity_hbm, diffusivity, load_sem.at[7]),
        pltpu.make_async_copy(label_hbm, LABEL, load_sem.at[0]),
        pltpu.make_async_copy(yield_hbm, YIELD, load_sem.at[1]),
        pltpu.make_async_copy(print_hbm, PRINT, load_sem.at[2]),
        pltpu.make_async_copy(b_hbm, B, load_sem.at[4]),
        pltpu.make_async_copy(warm_hbm, WARM, load_sem.at[3]),
    ]
    for load in loads:
        load.start()

    barrier = pltpu.get_barrier_semaphore()
    diagonal = [(x, y) for x in (down_x, up_x) for y in (down_y, up_y)]
    inside_c = [x & y for x in (has_lo_x, has_hi_x) for y in (has_lo_y, has_hi_y)]
    always = stages[0] + stages[1]
    greeted = list(zip(
        [(up_x, gy), (down_x, gy), (gx, up_y), (gx, down_y)] + diagonal,
        [has_hi_x, has_lo_x, has_hi_y, has_lo_y] + inside_c,
    ))

    def greet(partner):
        pl.semaphore_signal(barrier, inc=1, device_id=partner, device_id_type=MESH)

    for partner in always:
        greet(partner)
    for partner, inside in greeted:
        pl.when(inside)(functools.partial(greet, partner))
    answers = len(always) + sum(inside.astype(jnp.int32) for _, inside in greeted)

    for inside, halos in (
        (has_lo_x, (rx1_lo, rx2_lo, rx3_lo)),
        (has_hi_x, (rx1_hi, rx2_hi, rx3_hi)),
        (has_lo_y, (ry1_lo, ry2_lo, ry3_lo)),
        (has_hi_y, (ry1_hi, ry2_hi, ry3_hi)),
    ):
        @pl.when(jnp.logical_not(inside))
        def _():
            for halo in halos:
                halo[...] = jnp.zeros(halo.shape, jnp.float32)

    for k, inside in enumerate(inside_c):
        @pl.when(jnp.logical_not(inside))
        def _():
            rcorner[k] = jnp.zeros(rcorner.shape[1:], jnp.float32)

    row = lax.broadcasted_iota(jnp.int32, (ny, nz), 0)
    lane = lax.broadcasted_iota(jnp.int32, (ny, nz), 1)
    first_row, last_row = row == 0, row == ny - 1
    last_lane = lane == nz - 1
    edge_lane = (lane == 0) | last_lane

    def remote(src, dst, send, recv, partner):
        return pltpu.make_async_remote_copy(
            src_ref=src, dst_ref=dst, send_sem=send, recv_sem=recv,
            device_id=partner, device_id_type=MESH,
        )

    def start_faces(up, down, has_lo, has_hi):
        @pl.when(has_hi)
        def _():
            for copy in up:
                copy.start()

        @pl.when(has_lo)
        def _():
            for copy in down:
                copy.start()

    def finish_faces(up, down, has_lo, has_hi):
        @pl.when(has_hi)
        def _():
            for copy in up:
                copy.wait_send()
            for copy in down:
                copy.wait_recv()

        @pl.when(has_lo)
        def _():
            for copy in down:
                copy.wait_send()
            for copy in up:
                copy.wait_recv()

    def faces_y(ylo, yhi, rlo, rhi, send, recv):
        return (
            [remote(yhi, rlo, send.at[0], recv.at[0], (gx, up_y))],
            [remote(ylo, rhi, send.at[1], recv.at[1], (gx, down_y))],
            has_lo_y, has_hi_y,
        )

    def faces_x(field, rlo, rhi, send, recv):
        return (
            [remote(field.at[:, nx - 1], rlo, send.at[2], recv.at[2], (up_x, gy))],
            [remote(field.at[:, 0], rhi, send.at[3], recv.at[3], (down_x, gy))],
            has_lo_x, has_hi_x,
        )

    for load in loads[:-1]:
        load.wait()

    def properties(x, carry):
        label = LABEL[x]
        stiffness = (
            pick(rigidity, label)
            * (1.0 - 0.7 * YIELD[x].astype(jnp.float32))
            * (0.05 + 0.95 * PRINT[x].astype(jnp.float32))
        )
        half = 0.5 * stiffness
        H[x] = half
        at = pl.ds(x, 1)
        for c in range(3):
            y1_lo[c, at, :] = B[c, x, 0:1, :]
            y1_hi[c, at, :] = B[c, x, ny - 1 : ny, :]
        y1_lo[3, at, :] = half[0:1, :]
        y1_hi[3, at, :] = half[ny - 1 : ny, :]
        return carry

    lax.fori_loop(0, nx, properties, 0)

    corners = [(x, y) for x in (0, nx - 1) for y in (0, ny - 1)]
    for k, (x, y) in enumerate(corners):
        for c in range(3):
            corner[k, c : c + 1, :] = B[c, x, y : y + 1, :]
        corner[k, 3:4, :] = H[x, y : y + 1, :]

    pl.semaphore_wait(barrier, answers)

    copies_c = [
        remote(corner.at[k], rcorner.at[3 - k], send_c.at[k], recv_c.at[3 - k], partner)
        for k, partner in enumerate(diagonal)
    ]
    for copy, inside in zip(copies_c, inside_c):
        @pl.when(inside)
        def _():
            copy.start()

    copies1y = faces_y(y1_lo, y1_hi, ry1_lo, ry1_hi, send1, recv1)
    fields = pl.ds(0, 3)
    copies1x = (
        [
            remote(B.at[:, nx - 1], rx1_lo.at[fields], send1.at[2], recv1.at[2], (up_x, gy)),
            remote(H.at[nx - 1], rx1_lo.at[3], send1.at[4], recv1.at[4], (up_x, gy)),
        ],
        [
            remote(B.at[:, 0], rx1_hi.at[fields], send1.at[3], recv1.at[3], (down_x, gy)),
            remote(H.at[0], rx1_hi.at[3], send1.at[5], recv1.at[5], (down_x, gy)),
        ],
        has_lo_x, has_hi_x,
    )
    start_faces(*copies1y)
    start_faces(*copies1x)

    def next_y(plane):
        return pltpu.roll(plane, ny - 1, 0)

    def prev_y(plane):
        return pltpu.roll(plane, 1, 0)

    def next_z(plane):
        return pltpu.roll(plane, nz - 1, 1)

    def prev_z(plane):
        return pltpu.roll(plane, 1, 1)

    def inflow(field, c, x, here, wxm, wxp, wy, wz):
        total = wxp * (field[c, jnp.minimum(x + 1, nx - 1)] - here)
        total += wxm * (field[c, jnp.maximum(x - 1, 0)] - here)
        flux = wy * (next_y(here) - here)
        total += flux - prev_y(flux)
        flux = wz * (next_z(here) - here)
        return total + (flux - prev_z(flux))

    def weights_yz(half):
        wy = jnp.where(last_row, 0.0, half + next_y(half))
        wz = jnp.where(last_lane, 0.0, half + next_z(half))
        return wy, wz

    def weights_x(x, half):
        return half + H[jnp.maximum(x - 1, 0)], half + H[jnp.minimum(x + 1, nx - 1)]

    zero = jnp.zeros((8, 128), jnp.float32)

    def first_image(x, carry):
        bu, uu = carry
        at = pl.ds(x, 1)
        half = H[x]
        wxm, wxp = weights_x(x, half)
        wy, wz = weights_yz(half)
        diag = 0.5 + jnp.where(edge_lane, half, 0.0)
        WY[x], WZ[x], D[x] = wy, wz, diag
        for c in range(3):
            here = B[c, x]
            image = diag * here - inflow(B, c, x, here, wxm, wxp, wy, wz)
            U[c, x] = image
            y2_lo[c, at, :] = image[0:1, :]
            y2_hi[c, at, :] = image[ny - 1 : ny, :]
            bu += fold(here * image)
            uu += fold(image * image)
        return bu, uu

    bu, uu = lax.fori_loop(0, nx, first_image, (zero, zero))

    for c in range(3):
        x2_lo[c], x2_hi[c] = U[c, 0], U[c, nx - 1]
    copies2y = faces_y(y2_lo, y2_hi, ry2_lo, ry2_hi, send2, recv2)
    copies2x = (
        [remote(x2_hi, rx2_lo, send2.at[2], recv2.at[2], (up_x, gy))],
        [remote(x2_lo, rx2_hi, send2.at[3], recv2.at[3], (down_x, gy))],
        has_lo_x, has_hi_x,
    )
    start_faces(*copies2y)
    start_faces(*copies2x)
    for c in range(3):
        yu_lo[c], yu_hi[c] = y2_lo[c], y2_hi[c]

    loads[-1].wait()

    def thermal_properties(x, carry):
        label = LABEL[x]
        TS[x] = pick(dilatation, label) * (0.5 + WARM[x]) * H[x]
        half_c = 0.5 * pick(diffusivity, label)
        S3[2, x] = half_c
        at = pl.ds(x, 1)
        y3_lo[2, at, :] = half_c[0:1, :]
        y3_hi[2, at, :] = half_c[ny - 1 : ny, :]
        return carry

    lax.fori_loop(0, nx, thermal_properties, 0)

    finish_faces(*copies1x)
    for x, halo in ((0, rx1_lo), (nx - 1, rx1_hi)):
        weight = H[x] + halo[3]
        for c in range(3):
            here, image = B[c, x], U[c, x]
            more = weight * (here - halo[c])
            bu += fold(here * more)
            uu += fold(more * (2.0 * image + more))
            image += more
            U[c, x] = image
            yu_lo[c, x : x + 1, :] = image[0:1, :]
            yu_hi[c, x : x + 1, :] = image[ny - 1 : ny, :]
    finish_faces(*copies1y)
    for face, image, halo in ((y1_lo, yu_lo, ry1_lo), (y1_hi, yu_hi, ry1_hi)):
        weight = face[3] + halo[3]
        for c in range(3):
            more = weight * (face[c] - halo[c])
            bu += fold(face[c] * more)
            uu += fold(more * (2.0 * image[c] + more))
            image[c] = image[c] + more

    def set_rows(x, carry):
        at = pl.ds(x, 1)
        for c in range(3):
            U[c, x, 0:1, :] = yu_lo[c, at, :]
            U[c, x, ny - 1 : ny, :] = yu_hi[c, at, :]
        return carry

    lax.fori_loop(0, nx, set_rows, 0)

    def everywhere(tile):
        total = jnp.sum(jnp.sum(tile, axis=0, keepdims=True), axis=1, keepdims=True)
        return jnp.broadcast_to(total, (1, 128))

    weight = everywhere(uu)
    sigma = everywhere(bu) / jnp.where(weight > 0.0, weight, 1.0)
    sigma_all = jnp.broadcast_to(sigma[:, 0:1], (ny, nz))

    def second_image(x, carry):
        uu, rr, ru, rv, uv = carry
        half = H[x]
        wxm, wxp = weights_x(x, half)
        wy, wz, diag = WY[x], WZ[x], D[x]
        for c in range(3):
            here = U[c, x]
            image = diag * here - inflow(U, c, x, here, wxm, wxp, wy, wz)
            rest = B[c, x] - sigma_all * here
            uu += fold(here * here)
            rr += fold(rest * rest)
            ru += fold(rest * here)
            rv += fold(rest * image)
            uv += fold(here * image)
        return uu, rr, ru, rv, uv

    uu, rr, ru, rv, uv = lax.fori_loop(0, nx, second_image, (zero,) * 5)

    def source_of(field, xlo, xhi, rlo, rhi, out, ylo, yhi):
        def body(x, below, above):
            at = pl.ds(x, 1)
            mid, last = field[1, x], field[2, x]
            div = above - below
            div += jnp.where(last_row, rhi[1, at, :], next_y(mid))
            div -= jnp.where(first_row, rlo[1, at, :], prev_y(mid))
            div += jnp.where(last_lane, 0.0, next_z(last)) - jnp.where(lane == 0, 0.0, prev_z(last))
            source = -TS[x] * div
            S3[out, x] = source
            ylo[out, at, :] = source[0:1, :]
            yhi[out, at, :] = source[ny - 1 : ny, :]

        def inner(x, carry):
            body(x, field[0, x - 1], field[0, x + 1])
            return carry

        body(0, xlo[0], field[0, 1])
        lax.fori_loop(1, nx - 1, inner, 0)
        body(nx - 1, field[0, nx - 2], xhi[0])

    for k, inside in enumerate(inside_c):
        @pl.when(inside)
        def _():
            copies_c[k].wait_send()
            copies_c[3 - k].wait_recv()

    def complete(halo, field, own, low, high):
        weight = own(3) + field[3]
        for c in range(3):
            halo[c] = halo[c] + weight * (field[c] - own(c))
            for at, line in ((0, low), (field.shape[1] - 1, high)):
                at = slice(at, at + 1)
                edge = field[3, at, :] + rcorner[line, 3:4, :]
                edge = edge * (field[c, at, :] - rcorner[line, c : c + 1, :])
                halo[c, at, :] = halo[c, at, :] + edge

    finish_faces(*copies2x)
    for x, inside, halo, field, low, high in (
        (0, has_lo_x, rx2_lo, rx1_lo, 0, 1), (nx - 1, has_hi_x, rx2_hi, rx1_hi, 2, 3),
    ):
        @pl.when(inside)
        def _():
            complete(halo, field, lambda c: B[c, x] if c < 3 else H[x], low, high)

    for x, halo, stiff in ((0, rx2_lo, rx1_lo), (nx - 1, rx2_hi, rx1_hi)):
        weight = H[x] + stiff[3]
        for c in range(3):
            here = U[c, x]
            more = weight * (here - halo[c])
            rv += fold((B[c, x] - sigma_all * here) * more)
            uv += fold(here * more)
    finish_faces(*copies2y)
    for inside, halo, field, face, low, high in (
        (has_lo_y, ry2_lo, ry1_lo, y1_lo, 0, 2), (has_hi_y, ry2_hi, ry1_hi, y1_hi, 1, 3),
    ):
        @pl.when(inside)
        def _():
            complete(halo, field, lambda c: face[c], low, high)

    sigma_face = jnp.broadcast_to(sigma[:, 0:1], (nx, nz))
    for face, image, halo, stiff in ((y1_lo, yu_lo, ry2_lo, ry1_lo), (y1_hi, yu_hi, ry2_hi, ry1_hi)):
        weight = face[3] + stiff[3]
        for c in range(3):
            here = image[c]
            more = weight * (here - halo[c])
            rv += fold((face[c] - sigma_face * here) * more)
            uv += fold(here * more)

    def lanes(tile):
        return jnp.sum(tile, axis=0, keepdims=True)

    def pack(parts):
        index = lax.broadcasted_iota(jnp.int32, (8, 128), 0)
        tile = jnp.zeros((8, 128), jnp.float32)
        for i, part in enumerate(parts):
            tile = jnp.where(index == i, jnp.broadcast_to(part, (8, 128)), tile)
        return tile

    def merge(tiles):
        rows = [[tile[i : i + 1, :] for i in range(7)] for tile in tiles]
        weight = sum(r[6] for r in rows)
        sigma = sum(r[6] * r[5] for r in rows) / jnp.where(weight > 0.0, weight, 1.0)
        out = [0.0] * 5
        for uu, rr, ru, rv, uv, own, _ in rows:
            tau = own - sigma
            shifted = (
                uu, rr + tau * (2.0 * ru + tau * uu), ru + tau * uu, rv + tau * uv, uv,
            )
            out = [a + b for a, b in zip(out, shifted)]
        return out + [sigma, weight]

    weight = everywhere(uu)
    state = [lanes(m) for m in (uu, rr, ru, rv, uv)] + [sigma, weight]

    def reduce_start(stage, state):
        base = sum(len(s) for s in stages[:stage])
        own = sums.at[base + stage]
        sums[base + stage] = pack(state)
        copies = []
        for k, partner in enumerate(stages[stage]):
            copies.append(
                remote(own, sums.at[base + stage + 1 + k], send_r.at[base + k], recv_r.at[base + k], partner)
            )
        for copy in copies:
            copy.start()
        return copies

    def reduce_finish(stage, copies):
        base = sum(len(s) for s in stages[:stage]) + stage
        for copy in copies:
            copy.wait_recv()
        return merge([sums[base + k] for k in range(len(copies) + 1)])

    pending0 = reduce_start(0, state)
    source_of(B, rx1_lo, rx1_hi, ry1_lo, ry1_hi, 0, y3_lo, y3_hi)
    source_of(U, rx2_lo, rx2_hi, ry2_lo, ry2_hi, 1, y3_lo, y3_hi)
    copies3y = faces_y(y3_lo, y3_hi, ry3_lo, ry3_hi, send3, recv3)
    copies3x = faces_x(S3, rx3_lo, rx3_hi, send3, recv3)
    start_faces(*copies3y)
    start_faces(*copies3x)

    def conduct(x, carry):
        half = S3[2, x]
        wxm = half + S3[2, jnp.maximum(x - 1, 0)]
        wxp = half + S3[2, jnp.minimum(x + 1, nx - 1)]
        wy, wz = weights_yz(half)
        diag = 1.0 - 0.15 * jnp.where(edge_lane, half, 0.0)
        for c in range(2):
            here = S3[c, x]
            T[c, x] = diag * here + 0.15 * inflow(S3, c, x, here, wxm, wxp, wy, wz)
        return carry

    lax.fori_loop(0, nx, conduct, 0)
    state = reduce_finish(0, pending0)
    pending1 = reduce_start(1, state)

    finish_faces(*copies3x)
    for x, halo in ((0, rx3_lo), (nx - 1, rx3_hi)):
        weight = 0.15 * (S3[2, x] + halo[2])
        for c in range(2):
            T[c, x] = T[c, x] + weight * (halo[c] - S3[c, x])
    finish_faces(*copies3y)
    for face, halo in ((y3_lo, ry3_lo), (y3_hi, ry3_hi)):
        weight = 0.15 * (face[2] + halo[2])
        for c in range(2):
            halo[c] = weight * (halo[c] - face[c])

    def add_rows(x, carry):
        at = pl.ds(x, 1)
        for c in range(2):
            T[c, x, 0:1, :] = T[c, x, 0:1, :] + ry3_lo[c, at, :]
            T[c, x, ny - 1 : ny, :] = T[c, x, ny - 1 : ny, :] + ry3_hi[c, at, :]
        return carry

    lax.fori_loop(0, nx, add_rows, 0)
    for copy in pending0:
        copy.wait_send()
    state = reduce_finish(1, pending1)
    for copy in pending1:
        copy.wait_send()

    uu, rr, ru, rv, uv, sigma = [
        jnp.sum(part, axis=1, keepdims=True) for part in state[:5]
    ] + [state[5][:, 0:1]]
    energy = ru + sigma * uu
    norm = rr + sigma * (2.0 * ru + sigma * uu)
    step0 = norm / energy
    tau = sigma - step0
    norm1 = rr + tau * (2.0 * ru + tau * uu)
    ru, rv = ru + tau * uu, rv + tau * uv
    ratio = norm1 / norm
    curve = (ru - step0 * rv) + ratio * (2.0 * ru + ratio * energy)
    step1 = norm1 / curve
    coef_out[0:1, :] = jnp.broadcast_to(step0 + step1 * (1.0 + ratio), (1, 128))
    coef_out[1:2, :] = jnp.broadcast_to(-step1 * step0, (1, 128))


def combine(coef, b, u, t, x_hbm, th_hbm, x_out, th_out, sem):
    _, nx, ny, nz = b.shape
    coef_b = jnp.broadcast_to(coef[0:1, 0:1], (ny, nz))
    coef_u = jnp.broadcast_to(coef[1:2, 0:1], (ny, nz))
    copies = []
    chunk = nx // PIECES
    for piece in range(PIECES):
        for c in range(4):
            here = piece * chunk

            def one(x, carry):
                if c < 3:
                    x_out[c, x] = coef_b * b[c, x] + coef_u * u[c, x]
                else:
                    th_out[x] = coef_b * t[0, x] + coef_u * t[1, x]
                return carry

            lax.fori_loop(here, here + chunk, one, 0, unroll=True)
            planes = pl.ds(here, chunk)
            if c < 3:
                src, dst = x_out.at[c, planes], x_hbm.at[c, planes]
            else:
                src, dst = th_out.at[planes], th_hbm.at[planes]
            copies.append(pltpu.make_async_copy(src, dst, sem.at[len(copies)]))
            copies[-1].start()
    for copy in copies:
        copy.wait()


def per_device(*args):
    b = args[0]
    _, nx, ny, nz = b.shape
    gx_size, gy_size = lax.axis_size("gx"), lax.axis_size("gy")
    partners = sum(len(offset_partners(group, 0, 0, gx_size, gy_size)) for group in GROUPS)
    f32 = jnp.float32
    block = (nx, ny, nz)
    hbm, vmem = (pl.BlockSpec(memory_space=m) for m in (pltpu.HBM, pltpu.VMEM))
    dma = pltpu.SemaphoreType.DMA
    scratch = [pltpu.VMEM((3,) + block, f32)]
    scratch += [pltpu.VMEM(block, t) for t in [f32] * 2 + [jnp.int32] * 3 + [f32] * 4]
    scratch += [pltpu.VMEM((3,) + block, f32)]
    for fields in (4, 3, 3):
        scratch += [pltpu.VMEM((fields, nx, nz), f32)] * 4
        scratch += [pltpu.VMEM((fields, ny, nz), f32)] * 2
        if len(scratch) == 11 + 12:
            scratch += [pltpu.VMEM((3, ny, nz), f32)] * 2 + [pltpu.VMEM((3, nx, nz), f32)] * 2
    scratch += [pltpu.VMEM((4, 8, nz), f32)] * 2
    scratch += [pltpu.VMEM((partners + len(GROUPS), 8, 128), f32)]
    scratch += [pltpu.SMEM((4,), f32)] * 3
    scratch += [dma((8,))] + [dma((4,))] * 2 + [dma((6,))] * 2 + [dma((4,))] * 4 + [dma((partners,))] * 2
    u, t, coef = pl.pallas_call(
        functools.partial(kernel, gx_size, gy_size),
        out_shape=(
            jax.ShapeDtypeStruct((3,) + block, f32),
            jax.ShapeDtypeStruct((2,) + block, f32),
            jax.ShapeDtypeStruct((8, 128), f32),
        ),
        in_specs=[hbm] * 8,
        out_specs=(vmem, vmem, vmem),
        scratch_shapes=scratch,
        compiler_params=pltpu.CompilerParams(
            collective_id=0, has_side_effects=True, vmem_limit_bytes=40 * 1024 * 1024
        ),
        name="adjoint",
    )(*[pltpu.with_memory_space_constraint(arg, pltpu.HBM) for arg in args])
    return pl.pallas_call(
        combine,
        out_shape=(
            jax.ShapeDtypeStruct((3,) + block, f32), jax.ShapeDtypeStruct(block, f32),
        ),
        in_specs=[vmem] * 4,
        out_specs=(hbm, hbm),
        scratch_shapes=[
            pltpu.VMEM((3,) + block, f32), pltpu.VMEM(block, f32), dma((4 * PIECES,)),
        ],
        compiler_params=pltpu.CompilerParams(vmem_limit_bytes=16 * 1024 * 1024),
        name="combine",
    )(coef, b, u, t)


def solution(mesh):
    in_specs = (
        P(None, "gx", "gy", None),
        P("gx", "gy", None),
        P("gx", "gy", None),
        P("gx", "gy", None),
        P("gx", "gy", None),
        P(),
        P(),
        P(),
    )
    out_specs = (P(None, "gx", "gy", None), P("gx", "gy", None))
    return jax.shard_map(
        per_device, mesh=mesh, in_specs=in_specs, out_specs=out_specs, check_vma=False
    )
```

```python
import functools
import itertools

import jax
import jax.numpy as jnp
from jax import lax
from jax.experimental import pallas as pl
from jax.experimental.pallas import tpu as pltpu
from jax.sharding import PartitionSpec as P

MESH = pl.DeviceIdType.MESH
RING_X = 4


def pick(table, label):
    low = jnp.where(label == 0, table[0], table[1])
    high = jnp.where(label == 2, table[2], table[3])
    return jnp.where(label < 2, low, high)


def fold(plane):
    rows, lanes = plane.shape
    total = None
    for i in range(0, rows, 8):
        for j in range(0, lanes, 128):
            part = plane[i : i + 8, j : j + 128]
            total = part if total is None else total + part
    return total


GROUPS = ("cz", "xy")
PIECES = 2


def offset_partners(group, gx, gy, gx_size, gy_size):
    sizes = {"c": 2, "y": gx_size // 2, "z": gy_size // RING_X, "x": RING_X}
    place = {"c": gx % 2, "y": gx // 2, "z": gy // RING_X, "x": gy % RING_X}
    partners = []

    def hops(offsets):
        return sum(min(o, sizes[axis] - o) for axis, o in zip(group, offsets))

    every = itertools.product(*[range(sizes[axis]) for axis in group])
    for offsets in sorted(every, key=hops, reverse=True):
        if any(offsets):
            to = dict(place)
            for axis, offset in zip(group, offsets):
                to[axis] = (place[axis] + offset) % sizes[axis]
            partners.append((to["y"] * 2 + to["c"], to["z"] * RING_X + to["x"]))
    return partners


def kernel(
    gx_size, gy_size,
    b_hbm, warm_hbm, yield_hbm, print_hbm, label_hbm, rigidity_hbm, dilatation_hbm, diffusivity_hbm,
    U, T, coef_out, B,
    H, WARM, YIELD, PRINT, LABEL, TS, WY, WZ, D, S3,
    y1_lo, y1_hi, ry1_lo, ry1_hi, rx1_lo, rx1_hi,
    y2_lo, y2_hi, ry2_lo, ry2_hi, rx2_lo, rx2_hi, x2_lo, x2_hi, yu_lo, yu_hi,
    y3_lo, y3_hi, ry3_lo, ry3_hi, rx3_lo, rx3_hi,
    corner, rcorner, sums,
    rigidity, dilatation, diffusivity,
    load_sem, send_c, recv_c, send1, recv1, send2, recv2, send3, recv3, send_r, recv_r,
):
    _, nx, ny, nz = b_hbm.shape
    gx, gy = lax.axis_index("gx"), lax.axis_index("gy")
    ring_z = gy_size // RING_X
    gz, gq = gy // RING_X, gy % RING_X
    up_x, down_x = (gx + 1) % gx_size, (gx + gx_size - 1) % gx_size
    up_y, down_y = (gy + 1) % gy_size, (gy + gy_size - 1) % gy_size
    has_lo_x, has_hi_x = gx > 0, gx < gx_size - 1
    has_lo_y, has_hi_y = gy > 0, gy < gy_size - 1
    stages = [offset_partners(group, gx, gy, gx_size, gy_size) for group in GROUPS]

    loads = [
        pltpu.make_async_copy(rigidity_hbm, rigidity, load_sem.at[5]),
        pltpu.make_async_copy(dilatation_hbm, dilatation, load_sem.at[6]),
        pltpu.make_async_copy(diffusivity_hbm, diffusivity, load_sem.at[7]),
        pltpu.make_async_copy(label_hbm, LABEL, load_sem.at[0]),
        pltpu.make_async_copy(yield_hbm, YIELD, load_sem.at[1]),
        pltpu.make_async_copy(print_hbm, PRINT, load_sem.at[2]),
        pltpu.make_async_copy(b_hbm, B, load_sem.at[4]),
        pltpu.make_async_copy(warm_hbm, WARM, load_sem.at[3]),
    ]
    for load in loads:
        load.start()

    barrier = pltpu.get_barrier_semaphore()
    diagonal = [(x, y) for x in (down_x, up_x) for y in (down_y, up_y)]
    inside_c = [x & y for x in (has_lo_x, has_hi_x) for y in (has_lo_y, has_hi_y)]
    always = stages[0] + stages[1]
    greeted = list(zip(
        [(up_x, gy), (down_x, gy), (gx, up_y), (gx, down_y)] + diagonal,
        [has_hi_x, has_lo_x, has_hi_y, has_lo_y] + inside_c,
    ))

    def greet(partner):
        pl.semaphore_signal(barrier, inc=1, device_id=partner, device_id_type=MESH)

    for partner in always:
        greet(partner)
    for partner, inside in greeted:
        pl.when(inside)(functools.partial(greet, partner))
    answers = len(always) + sum(inside.astype(jnp.int32) for _, inside in greeted)

    for inside, halos in (
        (has_lo_x, (rx1_lo, rx2_lo, rx3_lo)),
        (has_hi_x, (rx1_hi, rx2_hi, rx3_hi)),
        (has_lo_y, (ry1_lo, ry2_lo, ry3_lo)),
        (has_hi_y, (ry1_hi, ry2_hi, ry3_hi)),
    ):
        @pl.when(jnp.logical_not(inside))
        def _():
            for halo in halos:
                halo[...] = jnp.zeros(halo.shape, jnp.float32)

    for k, inside in enumerate(inside_c):
        @pl.when(jnp.logical_not(inside))
        def _():
            rcorner[k] = jnp.zeros(rcorner.shape[1:], jnp.float32)

    row = lax.broadcasted_iota(jnp.int32, (ny, nz), 0)
    lane = lax.broadcasted_iota(jnp.int32, (ny, nz), 1)
    first_row, last_row = row == 0, row == ny - 1
    last_lane = lane == nz - 1
    edge_lane = (lane == 0) | last_lane

    def remote(src, dst, send, recv, partner):
        return pltpu.make_async_remote_copy(
            src_ref=src, dst_ref=dst, send_sem=send, recv_sem=recv,
            device_id=partner, device_id_type=MESH,
        )

    def start_faces(up, down, has_lo, has_hi):
        @pl.when(has_hi)
        def _():
            for copy in up:
                copy.start()

        @pl.when(has_lo)
        def _():
            for copy in down:
                copy.start()

    def finish_faces(up, down, has_lo, has_hi):
        @pl.when(has_hi)
        def _():
            for copy in up:
                copy.wait_send()
            for copy in down:
                copy.wait_recv()

        @pl.when(has_lo)
        def _():
            for copy in down:
                copy.wait_send()
            for copy in up:
                copy.wait_recv()

    def faces_y(ylo, yhi, rlo, rhi, send, recv):
        return (
            [remote(yhi, rlo, send.at[0], recv.at[0], (gx, up_y))],
            [remote(ylo, rhi, send.at[1], recv.at[1], (gx, down_y))],
            has_lo_y, has_hi_y,
        )

    def faces_x(field, rlo, rhi, send, recv):
        return (
            [remote(field.at[:, nx - 1], rlo, send.at[2], recv.at[2], (up_x, gy))],
            [remote(field.at[:, 0], rhi, send.at[3], recv.at[3], (down_x, gy))],
            has_lo_x, has_hi_x,
        )

    for load in loads[:-1]:
        load.wait()

    def properties(x, carry):
        label = LABEL[x]
        stiffness = (
            pick(rigidity, label)
            * (1.0 - 0.7 * YIELD[x].astype(jnp.float32))
            * (0.05 + 0.95 * PRINT[x].astype(jnp.float32))
        )
        half = 0.5 * stiffness
        H[x] = half
        at = pl.ds(x, 1)
        for c in range(3):
            y1_lo[c, at, :] = B[c, x, 0:1, :]
            y1_hi[c, at, :] = B[c, x, ny - 1 : ny, :]
        y1_lo[3, at, :] = half[0:1, :]
        y1_hi[3, at, :] = half[ny - 1 : ny, :]
        return carry

    lax.fori_loop(0, nx, properties, 0)

    corners = [(x, y) for x in (0, nx - 1) for y in (0, ny - 1)]
    for k, (x, y) in enumerate(corners):
        for c in range(3):
            corner[k, c : c + 1, :] = B[c, x, y : y + 1, :]
        corner[k, 3:4, :] = H[x, y : y + 1, :]

    pl.semaphore_wait(barrier, answers)

    copies_c = [
        remote(corner.at[k], rcorner.at[3 - k], send_c.at[k], recv_c.at[3 - k], partner)
        for k, partner in enumerate(diagonal)
    ]
    for copy, inside in zip(copies_c, inside_c):
        @pl.when(inside)
        def _():
            copy.start()

    copies1y = faces_y(y1_lo, y1_hi, ry1_lo, ry1_hi, send1, recv1)
    fields = pl.ds(0, 3)
    copies1x = (
        [
            remote(B.at[:, nx - 1], rx1_lo.at[fields], send1.at[2], recv1.at[2], (up_x, gy)),
            remote(H.at[nx - 1], rx1_lo.at[3], send1.at[4], recv1.at[4], (up_x, gy)),
        ],
        [
            remote(B.at[:, 0], rx1_hi.at[fields], send1.at[3], recv1.at[3], (down_x, gy)),
            remote(H.at[0], rx1_hi.at[3], send1.at[5], recv1.at[5], (down_x, gy)),
        ],
        has_lo_x, has_hi_x,
    )
    start_faces(*copies1y)
    start_faces(*copies1x)

    def next_y(plane):
        return pltpu.roll(plane, ny - 1, 0)

    def prev_y(plane):
        return pltpu.roll(plane, 1, 0)

    def next_z(plane):
        return pltpu.roll(plane, nz - 1, 1)

    def prev_z(plane):
        return pltpu.roll(plane, 1, 1)

    def inflow(field, c, x, here, wxm, wxp, wy, wz):
        total = wxp * (field[c, jnp.minimum(x + 1, nx - 1)] - here)
        total += wxm * (field[c, jnp.maximum(x - 1, 0)] - here)
        flux = wy * (next_y(here) - here)
        total += flux - prev_y(flux)
        flux = wz * (next_z(here) - here)
        return total + (flux - prev_z(flux))

    def weights_yz(half):
        wy = jnp.where(last_row, 0.0, half + next_y(half))
        wz = jnp.where(last_lane, 0.0, half + next_z(half))
        return wy, wz

    def weights_x(x, half):
        return half + H[jnp.maximum(x - 1, 0)], half + H[jnp.minimum(x + 1, nx - 1)]

    zero = jnp.zeros((8, 128), jnp.float32)

    def first_image(x, carry):
        bu, uu = carry
        at = pl.ds(x, 1)
        half = H[x]
        wxm, wxp = weights_x(x, half)
        wy, wz = weights_yz(half)
        diag = 0.5 + jnp.where(edge_lane, half, 0.0)
        WY[x], WZ[x], D[x] = wy, wz, diag
        for c in range(3):
            here = B[c, x]
            image = diag * here - inflow(B, c, x, here, wxm, wxp, wy, wz)
            U[c, x] = image
            y2_lo[c, at, :] = image[0:1, :]
            y2_hi[c, at, :] = image[ny - 1 : ny, :]
            bu += fold(here * image)
            uu += fold(image * image)
        return bu, uu

    bu, uu = lax.fori_loop(0, nx, first_image, (zero, zero))

    for c in range(3):
        x2_lo[c], x2_hi[c] = U[c, 0], U[c, nx - 1]
    copies2y = faces_y(y2_lo, y2_hi, ry2_lo, ry2_hi, send2, recv2)
    copies2x = (
        [remote(x2_hi, rx2_lo, send2.at[2], recv2.at[2], (up_x, gy))],
        [remote(x2_lo, rx2_hi, send2.at[3], recv2.at[3], (down_x, gy))],
        has_lo_x, has_hi_x,
    )
    start_faces(*copies2y)
    start_faces(*copies2x)
    for c in range(3):
        yu_lo[c], yu_hi[c] = y2_lo[c], y2_hi[c]

    loads[-1].wait()

    def thermal_properties(x, carry):
        label = LABEL[x]
        TS[x] = pick(dilatation, label) * (0.5 + WARM[x]) * H[x]
        half_c = 0.5 * pick(diffusivity, label)
        S3[2, x] = half_c
        at = pl.ds(x, 1)
        y3_lo[2, at, :] = half_c[0:1, :]
        y3_hi[2, at, :] = half_c[ny - 1 : ny, :]
        return carry

    lax.fori_loop(0, nx, thermal_properties, 0)

    finish_faces(*copies1x)
    for x, halo in ((0, rx1_lo), (nx - 1, rx1_hi)):
        weight = H[x] + halo[3]
        for c in range(3):
            here, image = B[c, x], U[c, x]
            more = weight * (here - halo[c])
            bu += fold(here * more)
            uu += fold(more * (2.0 * image + more))
            image += more
            U[c, x] = image
            yu_lo[c, x : x + 1, :] = image[0:1, :]
            yu_hi[c, x : x + 1, :] = image[ny - 1 : ny, :]
    finish_faces(*copies1y)
    for face, image, halo in ((y1_lo, yu_lo, ry1_lo), (y1_hi, yu_hi, ry1_hi)):
        weight = face[3] + halo[3]
        for c in range(3):
            more = weight * (face[c] - halo[c])
            bu += fold(face[c] * more)
            uu += fold(more * (2.0 * image[c] + more))
            image[c] = image[c] + more

    def set_rows(x, carry):
        at = pl.ds(x, 1)
        for c in range(3):
            U[c, x, 0:1, :] = yu_lo[c, at, :]
            U[c, x, ny - 1 : ny, :] = yu_hi[c, at, :]
        return carry

    lax.fori_loop(0, nx, set_rows, 0, unroll=4)

    def everywhere(tile):
        total = jnp.sum(jnp.sum(tile, axis=0, keepdims=True), axis=1, keepdims=True)
        return jnp.broadcast_to(total, (1, 128))

    total = everywhere(uu)
    sigma = everywhere(bu) / jnp.where(total > 0.0, total, 1.0)
    sigma_all = jnp.broadcast_to(sigma[:, 0:1], (ny, nz))

    def second_image(x, carry):
        rr, ru, rv, uv = carry
        half = H[x]
        wxm, wxp = weights_x(x, half)
        wy, wz, diag = WY[x], WZ[x], D[x]
        for c in range(3):
            here = U[c, x]
            image = diag * here - inflow(U, c, x, here, wxm, wxp, wy, wz)
            rest = B[c, x] - sigma_all * here
            rr += fold(rest * rest)
            ru += fold(rest * here)
            rv += fold(rest * image)
            uv += fold(here * image)
        return rr, ru, rv, uv

    rr, ru, rv, uv = lax.fori_loop(0, nx, second_image, (zero,) * 4, unroll=2)

    def source_of(field, xlo, xhi, rlo, rhi, out, ylo, yhi):
        def body(x, below, above):
            at = pl.ds(x, 1)
            mid, last = field[1, x], field[2, x]
            div = above - below
            div += jnp.where(last_row, rhi[1, at, :], next_y(mid))
            div -= jnp.where(first_row, rlo[1, at, :], prev_y(mid))
            div += jnp.where(last_lane, 0.0, next_z(last)) - jnp.where(lane == 0, 0.0, prev_z(last))
            source = -TS[x] * div
            S3[out, x] = source
            ylo[out, at, :] = source[0:1, :]
            yhi[out, at, :] = source[ny - 1 : ny, :]

        def inner(x, carry):
            body(x, field[0, x - 1], field[0, x + 1])
            return carry

        body(0, xlo[0], field[0, 1])
        lax.fori_loop(1, nx - 1, inner, 0)
        body(nx - 1, field[0, nx - 2], xhi[0])

    for k, inside in enumerate(inside_c):
        @pl.when(inside)
        def _():
            copies_c[k].wait_send()
            copies_c[3 - k].wait_recv()

    def complete(halo, field, own, low, high):
        weight = own(3) + field[3]
        for c in range(3):
            halo[c] = halo[c] + weight * (field[c] - own(c))
            for at, line in ((0, low), (field.shape[1] - 1, high)):
                at = slice(at, at + 1)
                edge = field[3, at, :] + rcorner[line, 3:4, :]
                edge = edge * (field[c, at, :] - rcorner[line, c : c + 1, :])
                halo[c, at, :] = halo[c, at, :] + edge

    finish_faces(*copies2x)
    for x, inside, halo, field, low, high in (
        (0, has_lo_x, rx2_lo, rx1_lo, 0, 1), (nx - 1, has_hi_x, rx2_hi, rx1_hi, 2, 3),
    ):
        @pl.when(inside)
        def _():
            complete(halo, field, lambda c: B[c, x] if c < 3 else H[x], low, high)

    for x, halo, stiff in ((0, rx2_lo, rx1_lo), (nx - 1, rx2_hi, rx1_hi)):
        weight = H[x] + stiff[3]
        for c in range(3):
            here = U[c, x]
            more = weight * (here - halo[c])
            rv += fold((B[c, x] - sigma_all * here) * more)
            uv += fold(here * more)
    finish_faces(*copies2y)
    for inside, halo, field, face, low, high in (
        (has_lo_y, ry2_lo, ry1_lo, y1_lo, 0, 2), (has_hi_y, ry2_hi, ry1_hi, y1_hi, 1, 3),
    ):
        @pl.when(inside)
        def _():
            complete(halo, field, lambda c: face[c], low, high)

    sigma_face = jnp.broadcast_to(sigma[:, 0:1], (nx, nz))
    for face, image, halo, stiff in ((y1_lo, yu_lo, ry2_lo, ry1_lo), (y1_hi, yu_hi, ry2_hi, ry1_hi)):
        weight = face[3] + stiff[3]
        for c in range(3):
            here = image[c]
            more = weight * (here - halo[c])
            rv += fold((face[c] - sigma_face * here) * more)
            uv += fold(here * more)

    def lanes(tile):
        return jnp.sum(tile, axis=0, keepdims=True)

    def pack(parts):
        index = lax.broadcasted_iota(jnp.int32, (8, 128), 0)
        tile = jnp.zeros((8, 128), jnp.float32)
        for i, part in enumerate(parts):
            tile = jnp.where(index == i, jnp.broadcast_to(part, (8, 128)), tile)
        return tile

    def merge(tiles):
        rows = [[tile[i : i + 1, :] for i in range(7)] for tile in tiles]
        weight = sum(r[6] for r in rows)
        sigma = sum(r[6] * r[5] for r in rows) / jnp.where(weight > 0.0, weight, 1.0)
        out = [0.0] * 5
        for uu, rr, ru, rv, uv, own, _ in rows:
            tau = own - sigma
            shifted = (
                uu, rr + tau * (2.0 * ru + tau * uu), ru + tau * uu, rv + tau * uv, uv,
            )
            out = [a + b for a, b in zip(out, shifted)]
        return out + [sigma, weight]

    state = [lanes(m) for m in (uu, rr, ru, rv, uv)] + [sigma, total]

    def reduce_start(stage, state):
        base = sum(len(s) for s in stages[:stage])
        own = sums.at[base + stage]
        sums[base + stage] = pack(state)
        copies = []
        for k, partner in enumerate(stages[stage]):
            copies.append(
                remote(own, sums.at[base + stage + 1 + k], send_r.at[base + k], recv_r.at[base + k], partner)
            )
        for copy in copies:
            copy.start()
        return copies

    def reduce_finish(stage, copies):
        base = sum(len(s) for s in stages[:stage]) + stage
        for copy in copies:
            copy.wait_recv()
        return merge([sums[base + k] for k in range(len(copies) + 1)])

    pending0 = reduce_start(0, state)
    source_of(B, rx1_lo, rx1_hi, ry1_lo, ry1_hi, 0, y3_lo, y3_hi)
    source_of(U, rx2_lo, rx2_hi, ry2_lo, ry2_hi, 1, y3_lo, y3_hi)
    copies3y = faces_y(y3_lo, y3_hi, ry3_lo, ry3_hi, send3, recv3)
    copies3x = faces_x(S3, rx3_lo, rx3_hi, send3, recv3)
    start_faces(*copies3y)
    start_faces(*copies3x)

    def conduct(x, carry):
        half = S3[2, x]
        wxm = half + S3[2, jnp.maximum(x - 1, 0)]
        wxp = half + S3[2, jnp.minimum(x + 1, nx - 1)]
        wy, wz = weights_yz(half)
        diag = 1.0 - 0.15 * jnp.where(edge_lane, half, 0.0)
        for c in range(2):
            here = S3[c, x]
            T[c, x] = diag * here + 0.15 * inflow(S3, c, x, here, wxm, wxp, wy, wz)
        return carry

    lax.fori_loop(0, nx, conduct, 0)
    state = reduce_finish(0, pending0)
    pending1 = reduce_start(1, state)

    finish_faces(*copies3x)
    for x, halo in ((0, rx3_lo), (nx - 1, rx3_hi)):
        weight = 0.15 * (S3[2, x] + halo[2])
        for c in range(2):
            T[c, x] = T[c, x] + weight * (halo[c] - S3[c, x])
    finish_faces(*copies3y)
    for face, halo in ((y3_lo, ry3_lo), (y3_hi, ry3_hi)):
        weight = 0.15 * (face[2] + halo[2])
        for c in range(2):
            halo[c] = weight * (halo[c] - face[c])

    def add_rows(x, carry):
        at = pl.ds(x, 1)
        for c in range(2):
            T[c, x, 0:1, :] = T[c, x, 0:1, :] + ry3_lo[c, at, :]
            T[c, x, ny - 1 : ny, :] = T[c, x, ny - 1 : ny, :] + ry3_hi[c, at, :]
        return carry

    lax.fori_loop(0, nx, add_rows, 0)
    for copy in pending0:
        copy.wait_send()
    state = reduce_finish(1, pending1)
    for copy in pending1:
        copy.wait_send()

    uu, rr, ru, rv, uv, sigma = [
        jnp.sum(part, axis=1, keepdims=True) for part in state[:5]
    ] + [state[5][:, 0:1]]
    energy = ru + sigma * uu
    norm = rr + sigma * (2.0 * ru + sigma * uu)
    step0 = norm / energy
    tau = sigma - step0
    norm1 = rr + tau * (2.0 * ru + tau * uu)
    ru, rv = ru + tau * uu, rv + tau * uv
    ratio = norm1 / norm
    curve = (ru - step0 * rv) + ratio * (2.0 * ru + ratio * energy)
    step1 = norm1 / curve
    coef_out[0:1, :] = jnp.broadcast_to(step0 + step1 * (1.0 + ratio), (1, 128))
    coef_out[1:2, :] = jnp.broadcast_to(-step1 * step0, (1, 128))


def combine(coef, b, u, t, x_hbm, th_hbm, x_out, th_out, sem):
    _, nx, ny, nz = b.shape
    coef_b = jnp.broadcast_to(coef[0:1, 0:1], (ny, nz))
    coef_u = jnp.broadcast_to(coef[1:2, 0:1], (ny, nz))
    copies = []
    chunk = nx // PIECES
    for piece in range(PIECES):
        for c in range(4):
            here = piece * chunk

            def one(x, carry):
                if c < 3:
                    x_out[c, x] = coef_b * b[c, x] + coef_u * u[c, x]
                else:
                    th_out[x] = coef_b * t[0, x] + coef_u * t[1, x]
                return carry

            lax.fori_loop(here, here + chunk, one, 0, unroll=True)
            planes = pl.ds(here, chunk)
            if c < 3:
                src, dst = x_out.at[c, planes], x_hbm.at[c, planes]
            else:
                src, dst = th_out.at[planes], th_hbm.at[planes]
            copies.append(pltpu.make_async_copy(src, dst, sem.at[len(copies)]))
            copies[-1].start()
    for copy in copies:
        copy.wait()


def per_device(*args):
    b = args[0]
    _, nx, ny, nz = b.shape
    gx_size, gy_size = lax.axis_size("gx"), lax.axis_size("gy")
    partners = sum(len(offset_partners(group, 0, 0, gx_size, gy_size)) for group in GROUPS)
    f32 = jnp.float32
    block = (nx, ny, nz)
    hbm, vmem = (pl.BlockSpec(memory_space=m) for m in (pltpu.HBM, pltpu.VMEM))
    dma = pltpu.SemaphoreType.DMA
    scratch = [pltpu.VMEM(block, t) for t in [f32] * 2 + [jnp.int32] * 3 + [f32] * 4]
    scratch += [pltpu.VMEM((3,) + block, f32)]
    for fields in (4, 3, 3):
        scratch += [pltpu.VMEM((fields, nx, nz), f32)] * 4
        scratch += [pltpu.VMEM((fields, ny, nz), f32)] * 2
        if len(scratch) == 10 + 12:
            scratch += [pltpu.VMEM((3, ny, nz), f32)] * 2 + [pltpu.VMEM((3, nx, nz), f32)] * 2
    scratch += [pltpu.VMEM((4, 8, nz), f32)] * 2
    scratch += [pltpu.VMEM((partners + len(GROUPS), 8, 128), f32)]
    scratch += [pltpu.SMEM((4,), f32)] * 3
    scratch += [dma((8,))] + [dma((4,))] * 2 + [dma((6,))] * 2 + [dma((4,))] * 4 + [dma((partners,))] * 2
    u, t, coef, b_here = pl.pallas_call(
        functools.partial(kernel, gx_size, gy_size),
        out_shape=(
            jax.ShapeDtypeStruct((3,) + block, f32),
            jax.ShapeDtypeStruct((2,) + block, f32),
            jax.ShapeDtypeStruct((8, 128), f32),
            jax.ShapeDtypeStruct((3,) + block, f32),
        ),
        in_specs=[hbm] * 8,
        out_specs=(vmem,) * 4,
        scratch_shapes=scratch,
        compiler_params=pltpu.CompilerParams(
            collective_id=0, has_side_effects=True, vmem_limit_bytes=40 * 1024 * 1024
        ),
        name="adjoint",
    )(*[pltpu.with_memory_space_constraint(arg, pltpu.HBM) for arg in args])
    return pl.pallas_call(
        combine,
        out_shape=(
            jax.ShapeDtypeStruct((3,) + block, f32), jax.ShapeDtypeStruct(block, f32),
        ),
        in_specs=[vmem] * 4,
        out_specs=(hbm, hbm),
        scratch_shapes=[
            pltpu.VMEM((3,) + block, f32), pltpu.VMEM(block, f32), dma((4 * PIECES,)),
        ],
        compiler_params=pltpu.CompilerParams(vmem_limit_bytes=16 * 1024 * 1024),
        name="combine",
    )(coef, b_here, u, t)


def solution(mesh):
    in_specs = (
        P(None, "gx", "gy", None),
        P("gx", "gy", None),
        P("gx", "gy", None),
        P("gx", "gy", None),
        P("gx", "gy", None),
        P(),
        P(),
        P(),
    )
    out_specs = (P(None, "gx", "gy", None), P("gx", "gy", None))
    return jax.shard_map(
        per_device, mesh=mesh, in_specs=in_specs, out_specs=out_specs, check_vma=False
    )
```

```python
import functools
import itertools

import jax
import jax.numpy as jnp
from jax import lax
from jax.experimental import pallas as pl
from jax.experimental.pallas import tpu as pltpu
from jax.sharding import PartitionSpec as P

MESH = pl.DeviceIdType.MESH
RING_X = 4


def pick(table, label):
    low = jnp.where(label == 0, table[0], table[1])
    high = jnp.where(label == 2, table[2], table[3])
    return jnp.where(label < 2, low, high)


def fold(plane):
    rows, lanes = plane.shape
    total = None
    for i in range(0, rows, 8):
        for j in range(0, lanes, 128):
            part = plane[i : i + 8, j : j + 128]
            total = part if total is None else total + part
    return total


GROUPS = ("cz", "xy")
PIECES = 2


def offset_partners(group, gx, gy, gx_size, gy_size):
    sizes = {"c": 2, "y": gx_size // 2, "z": gy_size // RING_X, "x": RING_X}
    place = {"c": gx % 2, "y": gx // 2, "z": gy // RING_X, "x": gy % RING_X}
    partners = []

    def hops(offsets):
        return sum(min(o, sizes[axis] - o) for axis, o in zip(group, offsets))

    every = itertools.product(*[range(sizes[axis]) for axis in group])
    for offsets in sorted(every, key=hops, reverse=True):
        if any(offsets):
            to = dict(place)
            for axis, offset in zip(group, offsets):
                to[axis] = (place[axis] + offset) % sizes[axis]
            partners.append((to["y"] * 2 + to["c"], to["z"] * RING_X + to["x"]))
    return partners


def kernel(
    gx_size, gy_size,
    b_hbm, warm_hbm, yield_hbm, print_hbm, label_hbm, rigidity_hbm, dilatation_hbm, diffusivity_hbm,
    U, T, coef_out, B,
    H, WARM, YIELD, PRINT, LABEL, TS, WY, WZ, D, S3,
    y1_lo, y1_hi, ry1_lo, ry1_hi, rx1_lo, rx1_hi,
    y2_lo, y2_hi, ry2_lo, ry2_hi, rx2_lo, rx2_hi, x2_lo, x2_hi, yu_lo, yu_hi,
    y3_lo, y3_hi, ry3_lo, ry3_hi, rx3_lo, rx3_hi,
    corner, rcorner, sums,
    rigidity, dilatation, diffusivity,
    load_sem, send_c, recv_c, send1, recv1, send2, recv2, send3, recv3, send_r, recv_r,
):
    _, nx, ny, nz = b_hbm.shape
    gx, gy = lax.axis_index("gx"), lax.axis_index("gy")
    ring_z = gy_size // RING_X
    gz, gq = gy // RING_X, gy % RING_X
    up_x, down_x = (gx + 1) % gx_size, (gx + gx_size - 1) % gx_size
    up_y, down_y = (gy + 1) % gy_size, (gy + gy_size - 1) % gy_size
    has_lo_x, has_hi_x = gx > 0, gx < gx_size - 1
    has_lo_y, has_hi_y = gy > 0, gy < gy_size - 1
    stages = [offset_partners(group, gx, gy, gx_size, gy_size) for group in GROUPS]

    loads = [
        pltpu.make_async_copy(rigidity_hbm, rigidity, load_sem.at[5]),
        pltpu.make_async_copy(dilatation_hbm, dilatation, load_sem.at[6]),
        pltpu.make_async_copy(diffusivity_hbm, diffusivity, load_sem.at[7]),
        pltpu.make_async_copy(label_hbm, LABEL, load_sem.at[0]),
        pltpu.make_async_copy(yield_hbm, YIELD, load_sem.at[1]),
        pltpu.make_async_copy(print_hbm, PRINT, load_sem.at[2]),
        pltpu.make_async_copy(b_hbm, B, load_sem.at[4]),
        pltpu.make_async_copy(warm_hbm, WARM, load_sem.at[3]),
    ]
    for load in loads:
        load.start()

    barrier = pltpu.get_barrier_semaphore()
    diagonal = [(x, y) for x in (down_x, up_x) for y in (down_y, up_y)]
    inside_c = [x & y for x in (has_lo_x, has_hi_x) for y in (has_lo_y, has_hi_y)]
    always = stages[0] + stages[1]
    greeted = list(zip(
        [(up_x, gy), (down_x, gy), (gx, up_y), (gx, down_y)] + diagonal,
        [has_hi_x, has_lo_x, has_hi_y, has_lo_y] + inside_c,
    ))

    def greet(partner):
        pl.semaphore_signal(barrier, inc=1, device_id=partner, device_id_type=MESH)

    for partner in always:
        greet(partner)
    for partner, inside in greeted:
        pl.when(inside)(functools.partial(greet, partner))
    answers = len(always) + sum(inside.astype(jnp.int32) for _, inside in greeted)

    for inside, halos in (
        (has_lo_x, (rx1_lo, rx2_lo, rx3_lo)),
        (has_hi_x, (rx1_hi, rx2_hi, rx3_hi)),
        (has_lo_y, (ry1_lo, ry2_lo, ry3_lo)),
        (has_hi_y, (ry1_hi, ry2_hi, ry3_hi)),
    ):
        @pl.when(jnp.logical_not(inside))
        def _():
            for halo in halos:
                halo[...] = jnp.zeros(halo.shape, jnp.float32)

    for k, inside in enumerate(inside_c):
        @pl.when(jnp.logical_not(inside))
        def _():
            rcorner[k] = jnp.zeros(rcorner.shape[1:], jnp.float32)

    row = lax.broadcasted_iota(jnp.int32, (ny, nz), 0)
    lane = lax.broadcasted_iota(jnp.int32, (ny, nz), 1)
    first_row, last_row = row == 0, row == ny - 1
    last_lane = lane == nz - 1
    edge_lane = (lane == 0) | last_lane

    def remote(src, dst, send, recv, partner):
        return pltpu.make_async_remote_copy(
            src_ref=src, dst_ref=dst, send_sem=send, recv_sem=recv,
            device_id=partner, device_id_type=MESH,
        )

    def start_faces(up, down, has_lo, has_hi):
        @pl.when(has_hi)
        def _():
            for copy in up:
                copy.start()

        @pl.when(has_lo)
        def _():
            for copy in down:
                copy.start()

    def finish_faces(up, down, has_lo, has_hi):
        @pl.when(has_hi)
        def _():
            for copy in up:
                copy.wait_send()
            for copy in down:
                copy.wait_recv()

        @pl.when(has_lo)
        def _():
            for copy in down:
                copy.wait_send()
            for copy in up:
                copy.wait_recv()

    def faces_y(ylo, yhi, rlo, rhi, send, recv):
        return (
            [remote(yhi, rlo, send.at[0], recv.at[0], (gx, up_y))],
            [remote(ylo, rhi, send.at[1], recv.at[1], (gx, down_y))],
            has_lo_y, has_hi_y,
        )

    def faces_x(field, rlo, rhi, send, recv):
        return (
            [remote(field.at[:, nx - 1], rlo, send.at[2], recv.at[2], (up_x, gy))],
            [remote(field.at[:, 0], rhi, send.at[3], recv.at[3], (down_x, gy))],
            has_lo_x, has_hi_x,
        )

    for load in loads[:-1]:
        load.wait()

    def properties(x, carry):
        label = LABEL[x]
        stiffness = (
            pick(rigidity, label)
            * (1.0 - 0.7 * YIELD[x].astype(jnp.float32))
            * (0.05 + 0.95 * PRINT[x].astype(jnp.float32))
        )
        half = 0.5 * stiffness
        H[x] = half
        at = pl.ds(x, 1)
        for c in range(3):
            y1_lo[c, at, :] = B[c, x, 0:1, :]
            y1_hi[c, at, :] = B[c, x, ny - 1 : ny, :]
        y1_lo[3, at, :] = half[0:1, :]
        y1_hi[3, at, :] = half[ny - 1 : ny, :]
        return carry

    lax.fori_loop(0, nx, properties, 0)

    corners = [(x, y) for x in (0, nx - 1) for y in (0, ny - 1)]
    for k, (x, y) in enumerate(corners):
        for c in range(3):
            corner[k, c : c + 1, :] = B[c, x, y : y + 1, :]
        corner[k, 3:4, :] = H[x, y : y + 1, :]

    pl.semaphore_wait(barrier, answers)

    copies_c = [
        remote(corner.at[k], rcorner.at[3 - k], send_c.at[k], recv_c.at[3 - k], partner)
        for k, partner in enumerate(diagonal)
    ]

    copies1y = faces_y(y1_lo, y1_hi, ry1_lo, ry1_hi, send1, recv1)
    fields = pl.ds(0, 3)
    copies1x = (
        [
            remote(B.at[:, nx - 1], rx1_lo.at[fields], send1.at[2], recv1.at[2], (up_x, gy)),
            remote(H.at[nx - 1], rx1_lo.at[3], send1.at[4], recv1.at[4], (up_x, gy)),
        ],
        [
            remote(B.at[:, 0], rx1_hi.at[fields], send1.at[3], recv1.at[3], (down_x, gy)),
            remote(H.at[0], rx1_hi.at[3], send1.at[5], recv1.at[5], (down_x, gy)),
        ],
        has_lo_x, has_hi_x,
    )
    start_faces(*copies1y)
    start_faces(*copies1x)
    for copy, inside in zip(copies_c, inside_c):
        @pl.when(inside)
        def _():
            copy.start()

    def next_y(plane):
        return pltpu.roll(plane, ny - 1, 0)

    def prev_y(plane):
        return pltpu.roll(plane, 1, 0)

    def next_z(plane):
        return pltpu.roll(plane, nz - 1, 1)

    def prev_z(plane):
        return pltpu.roll(plane, 1, 1)

    def inflow(field, c, x, here, wxm, wxp, wy, wz):
        total = wxp * (field[c, jnp.minimum(x + 1, nx - 1)] - here)
        total += wxm * (field[c, jnp.maximum(x - 1, 0)] - here)
        flux = wy * (next_y(here) - here)
        total += flux - prev_y(flux)
        flux = wz * (next_z(here) - here)
        return total + (flux - prev_z(flux))

    def weights_yz(half):
        wy = jnp.where(last_row, 0.0, half + next_y(half))
        wz = jnp.where(last_lane, 0.0, half + next_z(half))
        return wy, wz

    def weights_x(x, half):
        return half + H[jnp.maximum(x - 1, 0)], half + H[jnp.minimum(x + 1, nx - 1)]

    zero = jnp.zeros((8, 128), jnp.float32)

    def first_image(x, carry):
        bu, uu = carry
        at = pl.ds(x, 1)
        half = H[x]
        wxm, wxp = weights_x(x, half)
        wy, wz = weights_yz(half)
        diag = 0.5 + jnp.where(edge_lane, half, 0.0)
        WY[x], WZ[x], D[x] = wy, wz, diag
        for c in range(3):
            here = B[c, x]
            image = diag * here - inflow(B, c, x, here, wxm, wxp, wy, wz)
            U[c, x] = image
            y2_lo[c, at, :] = image[0:1, :]
            y2_hi[c, at, :] = image[ny - 1 : ny, :]
            bu += fold(here * image)
            uu += fold(image * image)
        return bu, uu

    bu, uu = lax.fori_loop(0, nx, first_image, (zero, zero))

    for c in range(3):
        x2_lo[c], x2_hi[c] = U[c, 0], U[c, nx - 1]
    copies2y = faces_y(y2_lo, y2_hi, ry2_lo, ry2_hi, send2, recv2)
    copies2x = (
        [remote(x2_hi, rx2_lo, send2.at[2], recv2.at[2], (up_x, gy))],
        [remote(x2_lo, rx2_hi, send2.at[3], recv2.at[3], (down_x, gy))],
        has_lo_x, has_hi_x,
    )
    start_faces(*copies2y)
    start_faces(*copies2x)
    for c in range(3):
        yu_lo[c], yu_hi[c] = y2_lo[c], y2_hi[c]

    loads[-1].wait()

    def thermal_properties(x, carry):
        label = LABEL[x]
        TS[x] = pick(dilatation, label) * (0.5 + WARM[x]) * H[x]
        half_c = 0.5 * pick(diffusivity, label)
        S3[2, x] = half_c
        at = pl.ds(x, 1)
        y3_lo[2, at, :] = half_c[0:1, :]
        y3_hi[2, at, :] = half_c[ny - 1 : ny, :]
        return carry

    lax.fori_loop(0, nx, thermal_properties, 0)

    finish_faces(*copies1x)
    for x, halo in ((0, rx1_lo), (nx - 1, rx1_hi)):
        weight = H[x] + halo[3]
        for c in range(3):
            here, image = B[c, x], U[c, x]
            more = weight * (here - halo[c])
            bu += fold(here * more)
            uu += fold(more * (2.0 * image + more))
            image += more
            U[c, x] = image
            yu_lo[c, x : x + 1, :] = image[0:1, :]
            yu_hi[c, x : x + 1, :] = image[ny - 1 : ny, :]
    finish_faces(*copies1y)
    for face, image, halo in ((y1_lo, yu_lo, ry1_lo), (y1_hi, yu_hi, ry1_hi)):
        weight = face[3] + halo[3]
        for c in range(3):
            more = weight * (face[c] - halo[c])
            bu += fold(face[c] * more)
            uu += fold(more * (2.0 * image[c] + more))
            image[c] = image[c] + more

    def set_rows(x, carry):
        at = pl.ds(x, 1)
        for c in range(3):
            U[c, x, 0:1, :] = yu_lo[c, at, :]
            U[c, x, ny - 1 : ny, :] = yu_hi[c, at, :]
        return carry

    lax.fori_loop(0, nx, set_rows, 0, unroll=4)

    def everywhere(tile):
        total = jnp.sum(jnp.sum(tile, axis=0, keepdims=True), axis=1, keepdims=True)
        return jnp.broadcast_to(total, (1, 128))

    total = everywhere(uu)
    sigma = everywhere(bu) / jnp.where(total > 0.0, total, 1.0)
    sigma_all = jnp.broadcast_to(sigma[:, 0:1], (ny, nz))

    def second_image(x, carry):
        rr, ru, rv, uv = carry
        half = H[x]
        wxm, wxp = weights_x(x, half)
        wy, wz, diag = WY[x], WZ[x], D[x]
        for c in range(3):
            here = U[c, x]
            image = diag * here - inflow(U, c, x, here, wxm, wxp, wy, wz)
            rest = B[c, x] - sigma_all * here
            rr += fold(rest * rest)
            ru += fold(rest * here)
            rv += fold(rest * image)
            uv += fold(here * image)
        return rr, ru, rv, uv

    rr, ru, rv, uv = lax.fori_loop(0, nx, second_image, (zero,) * 4, unroll=2)

    def source_of(field, xlo, xhi, rlo, rhi, out, ylo, yhi):
        def body(x, below, above):
            at = pl.ds(x, 1)
            mid, last = field[1, x], field[2, x]
            div = above - below
            div += jnp.where(last_row, rhi[1, at, :], next_y(mid))
            div -= jnp.where(first_row, rlo[1, at, :], prev_y(mid))
            div += jnp.where(last_lane, 0.0, next_z(last)) - jnp.where(lane == 0, 0.0, prev_z(last))
            source = -TS[x] * div
            S3[out, x] = source
            ylo[out, at, :] = source[0:1, :]
            yhi[out, at, :] = source[ny - 1 : ny, :]

        def inner(x, carry):
            body(x, field[0, x - 1], field[0, x + 1])
            return carry

        body(0, xlo[0], field[0, 1])
        lax.fori_loop(1, nx - 1, inner, 0)
        body(nx - 1, field[0, nx - 2], xhi[0])

    for k, inside in enumerate(inside_c):
        @pl.when(inside)
        def _():
            copies_c[k].wait_send()
            copies_c[3 - k].wait_recv()

    def complete(halo, field, own, low, high):
        weight = own(3) + field[3]
        for c in range(3):
            halo[c] = halo[c] + weight * (field[c] - own(c))
            for at, line in ((0, low), (field.shape[1] - 1, high)):
                at = slice(at, at + 1)
                edge = field[3, at, :] + rcorner[line, 3:4, :]
                edge = edge * (field[c, at, :] - rcorner[line, c : c + 1, :])
                halo[c, at, :] = halo[c, at, :] + edge

    finish_faces(*copies2x)
    for x, inside, halo, field, low, high in (
        (0, has_lo_x, rx2_lo, rx1_lo, 0, 1), (nx - 1, has_hi_x, rx2_hi, rx1_hi, 2, 3),
    ):
        @pl.when(inside)
        def _():
            complete(halo, field, lambda c: B[c, x] if c < 3 else H[x], low, high)

    for x, halo, stiff in ((0, rx2_lo, rx1_lo), (nx - 1, rx2_hi, rx1_hi)):
        weight = H[x] + stiff[3]
        for c in range(3):
            here = U[c, x]
            more = weight * (here - halo[c])
            rv += fold((B[c, x] - sigma_all * here) * more)
            uv += fold(here * more)
    finish_faces(*copies2y)
    for inside, halo, field, face, low, high in (
        (has_lo_y, ry2_lo, ry1_lo, y1_lo, 0, 2), (has_hi_y, ry2_hi, ry1_hi, y1_hi, 1, 3),
    ):
        @pl.when(inside)
        def _():
            complete(halo, field, lambda c: face[c], low, high)

    sigma_face = jnp.broadcast_to(sigma[:, 0:1], (nx, nz))
    for face, image, halo, stiff in ((y1_lo, yu_lo, ry2_lo, ry1_lo), (y1_hi, yu_hi, ry2_hi, ry1_hi)):
        weight = face[3] + stiff[3]
        for c in range(3):
            here = image[c]
            more = weight * (here - halo[c])
            rv += fold((face[c] - sigma_face * here) * more)
            uv += fold(here * more)

    def lanes(tile):
        return jnp.sum(tile, axis=0, keepdims=True)

    def pack(parts):
        index = lax.broadcasted_iota(jnp.int32, (8, 128), 0)
        tile = jnp.zeros((8, 128), jnp.float32)
        for i, part in enumerate(parts):
            tile = jnp.where(index == i, jnp.broadcast_to(part, (8, 128)), tile)
        return tile

    def merge(tiles):
        rows = [[tile[i : i + 1, :] for i in range(7)] for tile in tiles]
        weight = sum(r[6] for r in rows)
        sigma = sum(r[6] * r[5] for r in rows) / jnp.where(weight > 0.0, weight, 1.0)
        out = [0.0] * 5
        for uu, rr, ru, rv, uv, own, _ in rows:
            tau = own - sigma
            shifted = (
                uu, rr + tau * (2.0 * ru + tau * uu), ru + tau * uu, rv + tau * uv, uv,
            )
            out = [a + b for a, b in zip(out, shifted)]
        return out + [sigma, weight]

    state = [lanes(m) for m in (uu, rr, ru, rv, uv)] + [sigma, total]

    def reduce_start(stage, state):
        base = sum(len(s) for s in stages[:stage])
        own = sums.at[base + stage]
        sums[base + stage] = pack(state)
        copies = []
        for k, partner in enumerate(stages[stage]):
            copies.append(
                remote(own, sums.at[base + stage + 1 + k], send_r.at[base + k], recv_r.at[base + k], partner)
            )
        for copy in copies:
            copy.start()
        return copies

    def reduce_finish(stage, copies):
        base = sum(len(s) for s in stages[:stage]) + stage
        for copy in copies:
            copy.wait_recv()
        return merge([sums[base + k] for k in range(len(copies) + 1)])

    pending0 = reduce_start(0, state)
    source_of(B, rx1_lo, rx1_hi, ry1_lo, ry1_hi, 0, y3_lo, y3_hi)
    source_of(U, rx2_lo, rx2_hi, ry2_lo, ry2_hi, 1, y3_lo, y3_hi)
    copies3y = faces_y(y3_lo, y3_hi, ry3_lo, ry3_hi, send3, recv3)
    copies3x = faces_x(S3, rx3_lo, rx3_hi, send3, recv3)
    start_faces(*copies3y)
    start_faces(*copies3x)

    def conduct(x, carry):
        half = S3[2, x]
        wxm = half + S3[2, jnp.maximum(x - 1, 0)]
        wxp = half + S3[2, jnp.minimum(x + 1, nx - 1)]
        wy, wz = weights_yz(half)
        diag = 1.0 - 0.15 * jnp.where(edge_lane, half, 0.0)
        for c in range(2):
            here = S3[c, x]
            T[c, x] = diag * here + 0.15 * inflow(S3, c, x, here, wxm, wxp, wy, wz)
        return carry

    lax.fori_loop(0, nx, conduct, 0)
    state = reduce_finish(0, pending0)
    pending1 = reduce_start(1, state)

    finish_faces(*copies3x)
    for x, halo in ((0, rx3_lo), (nx - 1, rx3_hi)):
        weight = 0.15 * (S3[2, x] + halo[2])
        for c in range(2):
            T[c, x] = T[c, x] + weight * (halo[c] - S3[c, x])
    finish_faces(*copies3y)
    for face, halo in ((y3_lo, ry3_lo), (y3_hi, ry3_hi)):
        weight = 0.15 * (face[2] + halo[2])
        for c in range(2):
            halo[c] = weight * (halo[c] - face[c])

    def add_rows(x, carry):
        at = pl.ds(x, 1)
        for c in range(2):
            T[c, x, 0:1, :] = T[c, x, 0:1, :] + ry3_lo[c, at, :]
            T[c, x, ny - 1 : ny, :] = T[c, x, ny - 1 : ny, :] + ry3_hi[c, at, :]
        return carry

    lax.fori_loop(0, nx, add_rows, 0)
    for copy in pending0:
        copy.wait_send()
    state = reduce_finish(1, pending1)
    for copy in pending1:
        copy.wait_send()

    uu, rr, ru, rv, uv, sigma = [
        jnp.sum(part, axis=1, keepdims=True) for part in state[:5]
    ] + [state[5][:, 0:1]]
    energy = ru + sigma * uu
    norm = rr + sigma * (2.0 * ru + sigma * uu)
    step0 = norm / energy
    tau = sigma - step0
    norm1 = rr + tau * (2.0 * ru + tau * uu)
    ru, rv = ru + tau * uu, rv + tau * uv
    ratio = norm1 / norm
    curve = (ru - step0 * rv) + ratio * (2.0 * ru + ratio * energy)
    step1 = norm1 / curve
    coef_out[0:1, :] = jnp.broadcast_to(step0 + step1 * (1.0 + ratio), (1, 128))
    coef_out[1:2, :] = jnp.broadcast_to(-step1 * step0, (1, 128))


def combine(coef, b, u, t, x_hbm, th_hbm, x_out, th_out, sem):
    _, nx, ny, nz = b.shape
    coef_b = jnp.broadcast_to(coef[0:1, 0:1], (ny, nz))
    coef_u = jnp.broadcast_to(coef[1:2, 0:1], (ny, nz))
    copies = []
    chunk = nx // PIECES
    for piece in range(PIECES):
        for c in range(4):
            here = piece * chunk

            def one(x, carry):
                if c < 3:
                    x_out[c, x] = coef_b * b[c, x] + coef_u * u[c, x]
                else:
                    th_out[x] = coef_b * t[0, x] + coef_u * t[1, x]
                return carry

            lax.fori_loop(here, here + chunk, one, 0, unroll=True)
            planes = pl.ds(here, chunk)
            if c < 3:
                src, dst = x_out.at[c, planes], x_hbm.at[c, planes]
            else:
                src, dst = th_out.at[planes], th_hbm.at[planes]
            copies.append(pltpu.make_async_copy(src, dst, sem.at[len(copies)]))
            copies[-1].start()
    for copy in copies:
        copy.wait()


def per_device(*args):
    b = args[0]
    _, nx, ny, nz = b.shape
    gx_size, gy_size = lax.axis_size("gx"), lax.axis_size("gy")
    partners = sum(len(offset_partners(group, 0, 0, gx_size, gy_size)) for group in GROUPS)
    f32 = jnp.float32
    block = (nx, ny, nz)
    hbm, vmem = (pl.BlockSpec(memory_space=m) for m in (pltpu.HBM, pltpu.VMEM))
    dma = pltpu.SemaphoreType.DMA
    scratch = [pltpu.VMEM(block, t) for t in [f32] * 2 + [jnp.int32] * 3 + [f32] * 4]
    scratch += [pltpu.VMEM((3,) + block, f32)]
    for fields in (4, 3, 3):
        scratch += [pltpu.VMEM((fields, nx, nz), f32)] * 4
        scratch += [pltpu.VMEM((fields, ny, nz), f32)] * 2
        if len(scratch) == 10 + 12:
            scratch += [pltpu.VMEM((3, ny, nz), f32)] * 2 + [pltpu.VMEM((3, nx, nz), f32)] * 2
    scratch += [pltpu.VMEM((4, 8, nz), f32)] * 2
    scratch += [pltpu.VMEM((partners + len(GROUPS), 8, 128), f32)]
    scratch += [pltpu.SMEM((4,), f32)] * 3
    scratch += [dma((8,))] + [dma((4,))] * 2 + [dma((6,))] * 2 + [dma((4,))] * 4 + [dma((partners,))] * 2
    u, t, coef, b_here = pl.pallas_call(
        functools.partial(kernel, gx_size, gy_size),
        out_shape=(
            jax.ShapeDtypeStruct((3,) + block, f32),
            jax.ShapeDtypeStruct((2,) + block, f32),
            jax.ShapeDtypeStruct((8, 128), f32),
            jax.ShapeDtypeStruct((3,) + block, f32),
        ),
        in_specs=[hbm] * 8,
        out_specs=(vmem,) * 4,
        scratch_shapes=scratch,
        compiler_params=pltpu.CompilerParams(
            collective_id=0, has_side_effects=True, vmem_limit_bytes=40 * 1024 * 1024
        ),
        name="adjoint",
    )(*[pltpu.with_memory_space_constraint(arg, pltpu.HBM) for arg in args])
    return pl.pallas_call(
        combine,
        out_shape=(
            jax.ShapeDtypeStruct((3,) + block, f32), jax.ShapeDtypeStruct(block, f32),
        ),
        in_specs=[vmem] * 4,
        out_specs=(hbm, hbm),
        scratch_shapes=[
            pltpu.VMEM((3,) + block, f32), pltpu.VMEM(block, f32), dma((4 * PIECES,)),
        ],
        compiler_params=pltpu.CompilerParams(vmem_limit_bytes=16 * 1024 * 1024),
        name="combine",
    )(coef, b_here, u, t)


def solution(mesh):
    in_specs = (
        P(None, "gx", "gy", None),
        P("gx", "gy", None),
        P("gx", "gy", None),
        P("gx", "gy", None),
        P("gx", "gy", None),
        P(),
        P(),
        P(),
    )
    out_specs = (P(None, "gx", "gy", None), P("gx", "gy", None))
    return jax.shard_map(
        per_device, mesh=mesh, in_specs=in_specs, out_specs=out_specs, check_vma=False
    )
```
